32 devices in a mesh: dp: 8 (over y, x, core), expert: 4 (over z).
Axes of the slice: x: 2, y: 2, z: 4, core: 2. Of those that a mesh axis runs over, the one named last changes fastest.
Arguments:
- tokens: bfloat16 [8192, 1536], P(('dp', 'expert')), may hold values from -6 to 6
- cotangent: bfloat16 [8192, 1536], P(('dp', 'expert')), may hold values from -6 to 6
- norm_attn: bfloat16 [1536], P('dp'), may hold values from 0.5 to 1.5
- norm_moe: bfloat16 [1536], P('dp'), may hold values from 0.5 to 1.5
- w_query: bfloat16 [1536, 1536], P('dp'), may hold values from -0.3984375 to 0.3984375
- w_key: bfloat16 [1536, 512], P('dp'), may hold values from -0.3984375 to 0.3984375
- w_value: bfloat16 [1536, 512], P('dp'), may hold values from -0.15625 to 0.15625
- w_out: bfloat16 [1536, 1536], P('dp'), may hold values from -3 to 3
- w_router: bfloat16 [1536, 32], P('dp'), may hold values from -0.078125 to 0.078125
- w_gate: bfloat16 [1536, 32, 512], P(None, 'expert'), may hold values from -0.15625 to 0.15625
- w_up: bfloat16 [1536, 32, 512], P(None, 'expert'), may hold values from -0.15625 to 0.15625
- w_down: bfloat16 [1536, 32, 512], P(None, 'expert'), may hold values from -6 to 6
- routes: int32 [8192, 8], P(('dp', 'expert')), may hold values from 0 to 31, all different within a row; in each aligned block of 256 rows (0 to 255, 256 to 511, ...) at most 112 rows name the same one
Outputs:
- output: bfloat16 [8192, 1536], P(('dp', 'expert'))
- grad_tokens: bfloat16 [8192, 1536], P(('dp', 'expert'))
- grad_norm_attn: float32 [1536], P(('dp', 'expert'))
- grad_norm_moe: float32 [1536], P(('dp', 'expert'))
- grad_query: float32 [1536, 1536], P(('dp', 'expert'))
- grad_key: float32 [1536, 512], P(('dp', 'expert'))
- grad_value: float32 [1536, 512], P(('dp', 'expert'))
- grad_out: float32 [1536, 1536], P(('dp', 'expert'))
- grad_router: float32 [1536, 32], P(('dp', 'expert'))
- grad_gate: float32 [1536, 32, 512], P('dp', 'expert')
- grad_up: float32 [1536, 32, 512], P('dp', 'expert')
- grad_down: float32 [1536, 32, 512], P('dp', 'expert')
The draws below stay inside these ranges and needn't reach their ends.
Inputs may be any that keep to these rules, and one draw needn't show every extreme that they name: `routes`: each row names 8 different experts. Within the rows of one device (aligned blocks of 256 rows) no expert is named by more than 112 rows, and in every draw some expert is named by exactly 112 rows of some block.
All inputs are finite; a program needn't handle non-finite values.
Results may differ from the reference program's by a relative error of at most 0.02.
Values may be sent and summed in bfloat16 or wider, within the bound.
No kernel may reach another device: no remote copies, remote signals or barrier semaphores. Data moves between devices by JAX's collectives and lax.ppermute only.
A program may use at most 384 MiB of HBM per device.

```python
import functools
import math
import jax
import jax.numpy as jnp
import numpy as np
from jax import lax

D = 1536
HEADS = 24
KV_HEADS = 8
HEAD_DIM = 64
FF = 512
TOP = 8
EXPERTS = 32
LENGTH = 1024
ROWS = 256
CAP = 112
SEQS = 8
TOKENS = 8192
N_EXPERT = 4


def spiked(array, key, source, target, parts, factor):
    def block_of(position):
        return (jnp.arange(array.shape[position]) // (array.shape[position] // parts)).reshape((-1,) + (1,) * (array.ndim - 1 - position))

    one_side = jax.random.permutation(key, parts)[block_of(target)]
    other_side = (block_of(target) + parts // 2) % parts
    return jnp.where((block_of(source) == one_side) | (block_of(source) == other_side), factor * array, array)


def block_scale(rng, shape, cuts, smallest, high):
    level, own = 1.0, jax.random.fold_in(rng, 6)
    for axis_at, shards_of in cuts:
        heights = jnp.exp(jax.random.uniform(jax.random.fold_in(own, axis_at), (shards_of,), jnp.float32, smallest / len(cuts), high / len(cuts)))
        level = level * jnp.repeat(heights, shape[axis_at] // shards_of).reshape([-1 if axis == axis_at else 1 for axis in range(len(shape))])
    return level


def routed_block(own_key, own, number, rows, number_of, top, bound, skew):
    ranking = jax.random.permutation(own_key, number_of)
    crowded, usual = load_shares(number_of, rows * top, bound, skew, True), load_shares(number_of, rows * top, bound, skew, False)
    places = jnp.arange(number_of)

    def named(sizes, rotation):
        used = int((sizes > 0).sum())
        fixed = max(1, used // 4)
        shifted = fixed + (places - fixed + rotation * (used - fixed)) % max(1, number_of - fixed)
        return jnp.zeros((number_of,), jnp.int32).at[ranking[jnp.where(places < fixed, places, shifted)]].set(jnp.asarray(sizes, jnp.int32))

    sizes = jnp.where(number % 4 == 0, named(crowded, number // 4), named(usual, number - number // 4 - 1))
    mixed = jax.random.permutation(jax.random.fold_in(own, 3), number_of)
    giver, sink = mixed[0:number_of // 2 * 2:2], mixed[1:number_of // 2 * 2:2]
    slack = jnp.minimum(sizes[giver] - 1, bound - sizes[sink]) // 2
    slack = jnp.where((giver == ranking[0]) | (sink == ranking[0]) | (sizes[sink] == 0), 0, jnp.maximum(slack, 0))
    shifted = jax.random.randint(jax.random.fold_in(own, 4), (number_of // 2,), 0, 1 << 20) % (slack + 1)
    sizes = sizes.at[giver].add(-shifted).at[sink].add(shifted)
    labels = jnp.searchsorted(jnp.cumsum(sizes), jnp.arange(rows * top), side="right").astype(jnp.int32)
    listing = labels.reshape(top, rows).T
    listing = listing[jax.random.permutation(jax.random.fold_in(own, 1), rows)]
    rotation = jax.random.randint(jax.random.fold_in(own, 2), (rows, 1), 0, top)
    return jnp.take_along_axis(listing, (jnp.arange(top)[None, :] + rotation) % top, axis=1)


def load_shares(count, total, reach, slope, full):
    weights = [(1 << 20) // math.isqrt(rank ** slope) + 1 for rank in range(1, count + 1)]
    largest = reach if full else min(reach, max(-(-total // count), total * weights[0] // sum(weights)))
    least = 1 if total - largest >= count - 1 else 0
    given, spare = [largest] + [least] * (count - 1), total - largest - least * (count - 1)
    while spare > 0:
        movable = [i for i in range(1, count) if given[i] < largest] or [i for i in range(1, count) if given[i] < reach]
        mass, budget = sum([weights[i] for i in movable]), spare
        for i in movable:
            more = min(reach - given[i], max(1, budget * weights[i] // mass), spare)
            given[i] = given[i] + more
            spare = spare - more
    return np.array(given)


def centred(key, shape, scale, bound, cuts=(), kind=jnp.bfloat16):
    result = jax.random.normal(key, shape, jnp.float32) * scale
    if len(cuts) > 0:
        result = block_scale(key, shape, cuts, -0.22, 0.18) * result
    return jnp.clip(result, min=-bound, max=bound).astype(kind)


def heavy_noise(stream_key, extent, deviation, bound, shards, heavy, kind=jnp.bfloat16):
    values = deviation * jax.random.normal(stream_key, extent, jnp.float32)
    if shards:
        values = values * block_scale(stream_key, extent, shards, -0.22, 0.18)
    return jnp.clip(spiked(values, jax.random.fold_in(stream_key, 3), *heavy), -bound, bound).astype(kind)


def setup_inputs(seed: int = 0) -> dict:
    keys = jax.random.split(jax.random.key(seed), 14)
    tokens = heavy_noise(keys[0], (TOKENS, D), 1.0, 6.0, ((0, 32),), (0, 1, 32, 2.75))
    cotangent = centred(keys[1], (TOKENS, D), 1.0, 6.0, ((0, 32),))
    norm_attn = jnp.clip(1.0 + 0.1 * jax.random.normal(keys[2], (D,), jnp.float32), 0.5, 1.5).astype(jnp.bfloat16)
    norm_moe = jnp.clip(1.0 + 0.1 * jax.random.normal(keys[3], (D,), jnp.float32), 0.5, 1.5).astype(jnp.bfloat16)
    w_query = centred(keys[4], (D, HEADS * HEAD_DIM), 0.08, 0.3984375, ((0, 8),))
    w_key = centred(keys[5], (D, KV_HEADS * HEAD_DIM), 0.08, 0.3984375, ((0, 8),))
    w_value = centred(keys[6], (D, KV_HEADS * HEAD_DIM), D ** -0.5, 0.15625, ((0, 8),))
    w_out = centred(keys[7], (HEADS * HEAD_DIM, D), 0.5, 3.0, ((0, 8),))
    w_router = centred(keys[8], (D, EXPERTS), (4 * D) ** -0.5, 0.078125, ((0, 8),))
    w_gate = centred(keys[9], (D, EXPERTS, FF), D ** -0.5, 0.15625, ((1, 4),))
    w_up = centred(keys[10], (D, EXPERTS, FF), D ** -0.5, 0.15625, ((1, 4),))
    w_down = centred(keys[11], (D, EXPERTS, FF), 1.0, 6.0, ((1, 4),))
    routes_keys = jax.random.split(jax.random.fold_in(keys[12], 1), TOKENS // ROWS)
    routes_turns = jax.random.permutation(jax.random.fold_in(keys[12], 3), TOKENS // ROWS)
    routes = jax.vmap(lambda own, number: routed_block(jax.random.fold_in(keys[12], 2), own, number, ROWS, EXPERTS, TOP, CAP, 1))(routes_keys, routes_turns).reshape((TOKENS, TOP))
    return {"tokens": tokens, "cotangent": cotangent, "norm_attn": norm_attn, "norm_moe": norm_moe, "w_query": w_query, "w_key": w_key, "w_value": w_value, "w_out": w_out, "w_router": w_router, "w_gate": w_gate, "w_up": w_up, "w_down": w_down, "routes": routes}


FULL_PRECISION = lax.Precision.HIGHEST
RES_MULT = 0.22
ATT_MULT = 0.015625
NORM_EPS = 1e-06
ROPE_BASE = 10000.0

@jax.custom_vjp
def low(v):
    return lax.optimization_barrier(v.astype(jnp.bfloat16)).astype(jnp.float32)

@jax.custom_vjp
def low_back(v):
    return v

def low_keep(v):
    return (low(v), None)

def low_pass(kept, grad):
    return (grad,)

def back_keep(v):
    return (v, None)

def back_low(kept, grad):
    return (low(grad),)
low.defvjp(low_keep, low_pass)
low_back.defvjp(back_keep, back_low)

def inverse_rms(hidden):
    return lax.rsqrt(lax.optimization_barrier(jnp.mean(hidden * hidden, axis=-1, keepdims=True)) + NORM_EPS)

def rope_tables(positions, head_width):
    half_width = head_width // 2
    frequency = ROPE_BASE ** (-(jnp.arange(half_width, dtype=jnp.float32) * 2.0 / head_width))
    angles = positions.astype(jnp.float32)[:, None] * frequency[None, :]
    angles = jnp.concatenate([angles, angles], axis=1)
    return (jnp.cos(angles)[:, None, :], jnp.sin(angles)[:, None, :])

def rotate_half(values):
    half_width = values.shape[-1] // 2
    return jnp.concatenate([-values[..., half_width:], values[..., :half_width]], axis=-1)

def apply_rope(values, cos_table, sin_table):
    return values * cos_table + rotate_half(values) * sin_table

def route_slots(routes, experts):
    flat_routes = routes.reshape(-1)
    onehot = (flat_routes[:, None] == jnp.arange(experts, dtype=jnp.int32)[None, :]).astype(jnp.int32)
    earlier = jnp.cumsum(onehot, axis=0) - onehot
    return lax.optimization_barrier(jnp.sum(earlier * onehot, axis=1)).reshape(routes.shape)

def attention_block(hidden, norm_attn, w_query, w_key, w_value, w_out):
    positions = jnp.arange(LENGTH, dtype=jnp.int32)
    cos_table, sin_table = rope_tables(positions, HEAD_DIM)
    normed = low(hidden * inverse_rms(hidden) * norm_attn)
    query_pre = low_back(jnp.dot(normed, w_query, precision=FULL_PRECISION))
    key_pre = low_back(jnp.dot(normed, w_key, precision=FULL_PRECISION))
    value_rows = low_back(low(jnp.dot(normed, w_value, precision=FULL_PRECISION)))
    query_rope = low(apply_rope(query_pre.reshape(LENGTH, HEADS, HEAD_DIM), cos_table, sin_table))
    key_rope = low(apply_rope(key_pre.reshape(LENGTH, KV_HEADS, HEAD_DIM), cos_table, sin_table))
    query_four = query_rope.reshape(LENGTH, KV_HEADS, HEADS // KV_HEADS, HEAD_DIM)
    value_heads = value_rows.reshape(LENGTH, KV_HEADS, HEAD_DIM)
    scores = low_back(jnp.einsum('qhgd,khd->hgqk', query_four, key_rope, precision=FULL_PRECISION) * ATT_MULT)
    causal = positions[None, :] <= positions[:, None]
    scores = jnp.where(causal, scores, -1e+30)
    probability = low(jax.nn.softmax(scores, axis=-1))
    mixed_heads = jnp.einsum('hgqk,khd->qhgd', probability, value_heads, precision=FULL_PRECISION)
    attended = low_back(low(mixed_heads.reshape(LENGTH, HEADS * HEAD_DIM)))
    return low_back(jnp.dot(attended, w_out, precision=FULL_PRECISION))

def expert_block(normed, routes_seq, w_router, w_gate, w_up, w_down):
    logits = low_back(jnp.dot(normed, w_router, precision=FULL_PRECISION))
    gate_probs = jax.nn.softmax(jnp.take_along_axis(logits, routes_seq, axis=1), axis=1)
    blocks = routes_seq.reshape(N_EXPERT, ROWS, TOP)
    slot_pos = jax.vmap(functools.partial(route_slots, experts=EXPERTS))(blocks).reshape(LENGTH, TOP)
    block_index = (jnp.arange(LENGTH, dtype=jnp.int32) // ROWS)[:, None]
    target = (routes_seq * (N_EXPERT * CAP) + block_index * CAP + slot_pos).reshape(-1).astype(jnp.int32)
    repeated = jnp.repeat(normed, TOP, axis=0)
    slot_rows = jnp.zeros((EXPERTS * N_EXPERT * CAP, D), jnp.float32).at[target].add(repeated)
    received = low_back(slot_rows.reshape(EXPERTS, N_EXPERT * CAP, D))
    gate_pre = low_back(jnp.einsum('ecd,def->ecf', received, w_gate, precision=FULL_PRECISION))
    up_pre = low_back(jnp.einsum('ecd,def->ecf', received, w_up, precision=FULL_PRECISION))
    active = low(jax.nn.silu(gate_pre) * up_pre)
    expert_out = low_back(low(jnp.einsum('ecf,def->ecd', active, w_down, precision=FULL_PRECISION)))
    picked = expert_out.reshape(EXPERTS * N_EXPERT * CAP, D)[target].reshape(LENGTH, TOP, D)
    return lax.optimization_barrier(jnp.sum(picked * gate_probs[:, :, None], axis=1))

def layer_forward(tokens, norm_attn, norm_moe, w_query, w_key, w_value, w_out, w_router, w_gate, w_up, w_down, routes):

    def one_sequence(scan_carry, pieces):
        hidden, routes_seq = pieces
        middle = hidden + RES_MULT * attention_block(hidden, norm_attn, w_query, w_key, w_value, w_out)
        normed = low(middle * inverse_rms(middle) * norm_moe)
        output = middle + RES_MULT * expert_block(normed, routes_seq, w_router, w_gate, w_up, w_down)
        return (scan_carry, output)
    unused, outputs = lax.scan(jax.checkpoint(one_sequence), jnp.zeros((), jnp.float32), (tokens.reshape(SEQS, LENGTH, D), routes.reshape(SEQS, LENGTH, TOP)))
    return outputs.reshape(TOKENS, D)

def reference(tokens, cotangent, norm_attn, norm_moe, w_query, w_key, w_value, w_out, w_router, w_gate, w_up, w_down, routes):
    forward = functools.partial(layer_forward, routes=routes)
    output, pullback = jax.vjp(forward, tokens.astype(jnp.float32), norm_attn.astype(jnp.float32), norm_moe.astype(jnp.float32), w_query.astype(jnp.float32), w_key.astype(jnp.float32), w_value.astype(jnp.float32), w_out.astype(jnp.float32), w_router.astype(jnp.float32), w_gate.astype(jnp.float32), w_up.astype(jnp.float32), w_down.astype(jnp.float32))
    gradients = pullback(cotangent.astype(jnp.float32))
    return (output.astype(jnp.bfloat16), gradients[0].astype(jnp.bfloat16), gradients[1], gradients[2], gradients[3], gradients[4], gradients[5], gradients[6], gradients[7], gradients[8], gradients[9], gradients[10])
```

```python
import functools

import jax
import jax.numpy as jnp
from jax import lax
from jax.experimental import pallas as pl
from jax.experimental.pallas import tpu as pltpu
from jax.sharding import PartitionSpec as P

HEADS = 24
KV_HEADS = 8
HEAD_DIM = 64
TOP = 8
GROUP = HEADS // KV_HEADS
PAD = 128
PAIR = 2 * HEAD_DIM


RES_MULT = 0.22
ATT_MULT = 0.015625
NORM_EPS = 1e-06
ROPE_BASE = 10000.0
BF = jnp.bfloat16
F32 = jnp.float32


def dot(a, b, ca=1, cb=0):
    return lax.dot_general(a, b, (((ca,), (cb,)), ((), ())), preferred_element_type=F32)


def inverse_rms(hidden):
    return lax.rsqrt(jnp.mean(hidden * hidden, axis=-1, keepdims=True) + NORM_EPS)


def norm_back(hidden, inverse, gain_vector, grad_normed):
    weighted = grad_normed * gain_vector
    return inverse * weighted - hidden * inverse**3 * jnp.mean(
        weighted * hidden, axis=-1, keepdims=True
    )


def rope_tables(positions):
    half = HEAD_DIM // 2
    frequency = ROPE_BASE ** (-(jnp.arange(half, dtype=F32) * 2.0 / HEAD_DIM))
    angles = positions.astype(F32)[:, None] * frequency[None, :]
    cos, sin = jnp.cos(angles), jnp.sin(angles)
    return jnp.concatenate([cos] * 4, axis=1), jnp.concatenate([-sin, sin] * 2, axis=1)


def swap_halves(x):
    half = HEAD_DIM // 2
    lane = lax.broadcasted_iota(jnp.int32, x.shape, 1)
    return jnp.where(
        lane % HEAD_DIM < half, pltpu.roll(x, PAIR - half, 1), pltpu.roll(x, half, 1)
    )


def rope(x, cos, sin):
    return jnp.concatenate(
        [
            x[:, i : i + PAIR] * cos + swap_halves(x[:, i : i + PAIR]) * sin
            for i in range(0, x.shape[1], PAIR)
        ],
        axis=1,
    )


def causal_bias(me, count, rows):
    query = me * rows + lax.broadcasted_iota(jnp.int32, (rows, count * rows), 0)
    key = lax.broadcasted_iota(jnp.int32, (rows, count * rows), 1)
    source = me - key // rows
    source = jnp.where(source < 0, source + count, source)
    return jnp.where(source * rows + key % rows <= query, 0.0, -1e30)


def front_kernel(count, gain_at, me_ref, *refs):
    token_refs = refs[:count]
    wq_ref, wk_ref, wv_ref, side_ref, cos_ref, sin_ref = refs[count : count + 6]
    normed_ref, side_out, q_ref, k_ref, v_ref, att_ref, lse_ref, bias_ref = refs[count + 6 :]
    rows = token_refs[0].shape[0]

    @pl.when(pl.program_id(0) == 0)
    def _():
        side = side_ref[...].astype(F32).T
        side_out[...] = side
        for s in range(count):
            hidden = token_refs[s][...].astype(F32)
            normed = hidden * inverse_rms(hidden) * side[gain_at : gain_at + 1]
            normed_ref[s * rows : (s + 1) * rows] = normed.astype(BF)
        bias_ref[...] = causal_bias(me_ref[0], count, rows)

    cos, sin = cos_ref[...], sin_ref[...]
    query = rope(dot(normed_ref[:rows], wq_ref[...]), cos[:rows], sin[:rows]).astype(BF)
    query = query * ATT_MULT
    q_ref[...] = query
    both = dot(normed_ref[...], jnp.concatenate([wk_ref[...], wv_ref[...]], axis=1))
    key = rope(both[:, :PAIR], cos, sin).astype(BF)
    value = both[:, PAIR:].astype(BF)
    k_ref[...] = key
    v_ref[...] = value
    lse_ref[...] = jnp.zeros_like(lse_ref)
    for head in range(2 * GROUP):
        at = slice(head * HEAD_DIM, (head + 1) * HEAD_DIM)
        kv_at = slice(head // GROUP * HEAD_DIM, (head // GROUP + 1) * HEAD_DIM)
        scores = dot(query[:, at], key[:, kv_at], 1, 1) + bias_ref[...]
        peak = jnp.max(scores, axis=1, keepdims=True)
        weight = jnp.exp(scores - peak)
        total = jnp.sum(weight, axis=1, keepdims=True)
        probs = (weight * (1.0 / total)).astype(BF)
        att_ref[:, at] = dot(probs, value[:, kv_at]).astype(BF)
        lse_ref[:, head : head + 1] = peak + jnp.log(total)


def run_front(me, tokens, full, cos, sin, query_width, key_width, gain_at):
    count, (rows, width) = len(tokens), tokens[0].shape
    length, pairs, wide = count * rows, key_width // PAIR, GROUP * PAIR
    whole = lambda shape: pl.BlockSpec(shape, lambda p, i: (0, 0))
    column = lambda r, w, first: pl.BlockSpec((r, w), lambda p, i: (0, first + p))
    flops = 2 * width * (rows * query_width + 2 * length * key_width)
    flops += 4 * rows * length * query_width
    return pl.pallas_call(
        functools.partial(front_kernel, count, gain_at),
        grid_spec=pltpu.PrefetchScalarGridSpec(
            num_scalar_prefetch=1,
            grid=(pairs,),
            in_specs=[whole((rows, width))] * count
            + [
                column(width, wide, 0),
                column(width, PAIR, query_width // PAIR),
                column(width, PAIR, (query_width + key_width) // PAIR),
                pl.BlockSpec(
                    (width, PAIR), lambda p, i: (0, (query_width + 2 * key_width) // PAIR)
                ),
                whole((length, PAIR)),
                whole((length, PAIR)),
            ],
            out_specs=[
                whole((length, width)),
                whole((PAIR, width)),
                column(rows, wide, 0),
                column(length, PAIR, 0),
                column(length, PAIR, 0),
                column(rows, wide, 0),
                column(rows, PAIR, 0),
            ],
            scratch_shapes=[pltpu.VMEM((rows, length), F32)],
        ),
        out_shape=[
            jax.ShapeDtypeStruct((length, width), BF),
            jax.ShapeDtypeStruct((PAIR, width), F32),
            jax.ShapeDtypeStruct((rows, query_width), BF),
            jax.ShapeDtypeStruct((length, key_width), BF),
            jax.ShapeDtypeStruct((length, key_width), BF),
            jax.ShapeDtypeStruct((rows, query_width), BF),
            jax.ShapeDtypeStruct((rows, pairs * PAIR), F32),
        ],
        compiler_params=pltpu.CompilerParams(
            dimension_semantics=("arbitrary",), vmem_limit_bytes=56 * 2**20
        ),
        cost_estimate=pl.CostEstimate(
            flops=flops,
            bytes_accessed=4 * (length * width + full.size),
            transcendentals=rows * length * query_width // HEAD_DIM,
        ),
        name="front",
    )(me, *tokens, full, full, full, full, cos, sin)


def back_kernel(count, me_ref, *refs):
    branch_ref, wo_ref, q_ref, k_ref, v_ref, lse_ref, cos_ref, sin_ref, normed_ref = refs[:9]
    dq_ref, dk_ref, dv_ref, keep_ref, send_ref, bias_ref = refs[9:]
    rows = branch_ref.shape[0]

    @pl.when(pl.program_id(0) == 0)
    def _():
        bias_ref[...] = causal_bias(me_ref[0], count, rows)

    grad = dot(branch_ref[...], wo_ref[...], 1, 1).astype(BF)
    query, key, value = q_ref[...], k_ref[...], v_ref[...]
    dqs, dks, dvs = [], [], []
    for head in range(2 * GROUP):
        at = slice(head * HEAD_DIM, (head + 1) * HEAD_DIM)
        kv_at = slice(head // GROUP * HEAD_DIM, (head // GROUP + 1) * HEAD_DIM)
        scores = dot(query[:, at], key[:, kv_at], 1, 1) + bias_ref[...]
        probs = jnp.exp(scores - lse_ref[:, head : head + 1])
        probs_back = dot(grad[:, at], value[:, kv_at], 1, 1)
        delta = jnp.sum(probs * probs_back, axis=1, keepdims=True)
        scores_back = (probs * (probs_back - delta)).astype(BF)
        dqs.append(dot(scores_back, key[:, kv_at]) * ATT_MULT)
        dk = dot(scores_back, query[:, at], 0, 0)
        dv = dot(probs.astype(BF), grad[:, at], 0, 0)
        if head % GROUP == 0:
            dks.append(dk)
            dvs.append(dv)
        else:
            dks[-1] = dks[-1] + dk
            dvs[-1] = dvs[-1] + dv
    cos, sin = cos_ref[...], sin_ref[...]
    dq = rope(jnp.concatenate(dqs, axis=1), cos[:rows], -sin[:rows]).astype(BF)
    dk = rope(jnp.concatenate(dks, axis=1), cos, -sin).astype(BF)
    dv = jnp.concatenate(dvs, axis=1).astype(BF)
    dq_ref[...] = dq
    dk_ref[...] = dk
    dv_ref[...] = dv
    wide = dq.shape[1]
    grad_q = dot(normed_ref[:, :rows], dq).astype(BF)
    grad_kv = dot(normed_ref[...], jnp.concatenate([dk, dv], axis=1)).astype(BF)
    store_slabs(keep_ref, send_ref, me_ref[1], slice(0, wide), grad_q)
    store_slabs(keep_ref, send_ref, me_ref[1], slice(wide, wide + 2 * PAIR), grad_kv)


def out_kernel(total, me_ref, att_ref, branch_ref, normed_ref, logit_ref, gain_ref, *grad_refs):
    width = branch_ref.shape[1]
    router = dot(normed_ref[...].T, logit_ref[...])
    gain = jnp.broadcast_to(gain_ref[0:1], (PAD, width)).T
    lane = lax.broadcasted_iota(jnp.int32, (width, PAD), 1)
    side = jnp.where(lane == total, gain, router).astype(BF)
    main = dot(att_ref[...].T, branch_ref[...]).astype(BF)
    store_slabs(*grad_refs, me_ref[1], slice(0, width), main)
    store_slabs(*grad_refs, me_ref[1], slice(width, width + PAD), side)


def run_out(me, attended, branch, normed, logits, gain, slabs, total):
    rows, width = branch.shape
    inner = attended.shape[1]
    spec = pl.BlockSpec(memory_space=pltpu.VMEM)
    return pl.pallas_call(
        functools.partial(out_kernel, total),
        in_specs=[pl.BlockSpec(memory_space=pltpu.SMEM)] + [spec] * 5,
        out_specs=[spec] * 2,
        out_shape=[jax.ShapeDtypeStruct((slabs // 2, inner // slabs, width + PAD), BF)] * 2,
        compiler_params=pltpu.CompilerParams(vmem_limit_bytes=48 * 2**20),
        cost_estimate=pl.CostEstimate(
            flops=2 * rows * inner * (width + PAD),
            bytes_accessed=2 * (3 * rows * width + inner * (width + PAD)),
            transcendentals=0,
        ),
        name="out_grad",
    )(me, attended, branch, normed, logits, gain)


def run_back(me, branch, out_full, query, key, value, lse, cos, sin, normed_t, slabs):
    (rows, width), (length, key_width) = branch.shape, key.shape
    count, pairs, wide = length // rows, key_width // PAIR, GROUP * PAIR
    whole = lambda shape: pl.BlockSpec(shape, lambda p, i: (0, 0))
    column = lambda r, w: pl.BlockSpec((r, w), lambda p, i: (0, p))
    flops = 2 * width * (2 * rows * query.shape[1] + 2 * length * key_width)
    flops += 10 * rows * length * query.shape[1]
    return pl.pallas_call(
        functools.partial(back_kernel, count),
        grid_spec=pltpu.PrefetchScalarGridSpec(
            num_scalar_prefetch=1,
            grid=(pairs,),
            in_specs=[
                whole((rows, width)),
                pl.BlockSpec((wide, width), lambda p, i: (p, 0)),
                column(rows, wide),
                column(length, PAIR),
                column(length, PAIR),
                column(rows, PAIR),
                whole((length, PAIR)),
                whole((length, PAIR)),
                whole((width, length)),
            ],
            out_specs=[
                column(rows, wide),
                column(length, PAIR),
                column(length, PAIR),
            ]
            + [pl.BlockSpec((slabs // 2, width // slabs, wide + 2 * PAIR), lambda p, i: (0, 0, p))]
            * 2,
            scratch_shapes=[pltpu.VMEM((rows, length), F32)],
        ),
        out_shape=[
            jax.ShapeDtypeStruct(query.shape, BF),
            jax.ShapeDtypeStruct(key.shape, BF),
            jax.ShapeDtypeStruct(key.shape, BF),
        ]
        + [jax.ShapeDtypeStruct((slabs // 2, width // slabs, pairs * (wide + 2 * PAIR)), BF)] * 2,
        compiler_params=pltpu.CompilerParams(
            dimension_semantics=("arbitrary",), vmem_limit_bytes=56 * 2**20
        ),
        cost_estimate=pl.CostEstimate(
            flops=flops,
            bytes_accessed=2 * (length * width + 2 * width * query.shape[1]),
            transcendentals=rows * length * query.shape[1] // HEAD_DIM,
        ),
        name="back",
    )(me, branch, out_full, query, key, value, lse, cos, sin, normed_t)


def line_gather(block, axis, count):
    right, left = [block], [block]
    for step in range(1, count):
        right.append(
            lax.ppermute(right[-1], axis, [(i, i + 1) for i in range(step - 1, count - 1)])
        )
        left.append(lax.ppermute(left[-1], axis, [(i, i - 1) for i in range(1, count - step + 1)]))
    return [block] + [right[s] + left[count - s] for s in range(1, count)]


def line_scatter(parts, axis, count):
    if count == 1:
        return parts[0].astype(F32)
    right, left = parts[1], parts[count - 1]
    for step in range(1, count):
        right = lax.ppermute(right, axis, [(i, i + 1) for i in range(step)])
        left = lax.ppermute(left, axis, [(i, i - 1) for i in range(count - step, count)])
        if step < count - 1:
            right = parts[step + 1] + right
            left = parts[count - 1 - step] + left
    return parts[0].astype(F32) + right.astype(F32) + left.astype(F32)


def upward(block, axis, count, distance=1, first=0):
    pairs = [(i, i + distance) for i in range(first, count - distance)]
    return lax.ppermute(block, axis, pairs)


def downward(block, axis, count, distance=1, last=0):
    pairs = [(i, i - distance) for i in range(distance, count - last)]
    return lax.ppermute(block, axis, pairs)


def send_parts(parts, axis, count):
    return [
        lax.ppermute(parts[s], axis, [(i, (i + count - s) % count) for i in range(count)])
        for s in range(1, count)
    ]


def send_near(parts, axis, count):
    shifts = [s for s in {1: 1, count - 1: 1} if 0 < s < count]
    return [
        lax.ppermute(parts[s], axis, [(i, (i + count - s) % count) for i in range(count)])
        for s in shifts
    ]


def send_far(parts, axis, count):
    return [
        lax.ppermute(part, axis, [(i, (i + count - s) % count) for i in range(count)])
        for s, part in enumerate(parts, 2)
    ]


def add_up(parts):
    total = parts[0].astype(F32)
    for part in parts[1:]:
        total = total + part.astype(F32)
    return total


def trade(keep, send, bit, slabs):
    return keep + lax.ppermute(send, "dp", [(i, i ^ (1 << bit)) for i in range(slabs)])


def halve(x, bits, bit, slabs):
    at = bits.index(bit)
    keep, send = (lax.index_in_dim(x, i, at, False) for i in (0, 1))
    return trade(keep, send, bit, slabs), [b for b in bits if b != bit]


def slab_stages(x, slabs):
    top = slabs.bit_length() - 1
    bits = list(range(top - 1, 0, -1))
    x = x.reshape((2,) * (top - 1) + x.shape[1:])
    one, two = jnp.split(x, 2, axis=len(bits))
    bits_one, bits_two = bits, bits
    for k in range(len(bits)):
        one, bits_one = halve(one, bits_one, k + 1, slabs)
        two, bits_two = halve(two, bits_two, len(bits) - k, slabs)
        one, two = yield one, two


def own_parts(one, two, me, count):
    x = jnp.concatenate([one, two], axis=0)
    own = x.shape[0] // count
    return [
        lax.dynamic_slice_in_dim(x, lax.rem(me + count - s, count) * own, own, 0)
        for s in range(count)
    ]


def store_slabs(keep_ref, send_ref, own, at, value):
    half, slab, _ = keep_ref.shape
    for odd in (0, 1):

        @pl.when(lax.rem(own, 2) == odd)
        def _():
            for d in range(2 * half):
                ref = keep_ref if d % 2 == odd else send_ref
                place = lax.bitwise_xor(jnp.int32(d), own) // 2
                ref[place, :, at] = value[d * slab : (d + 1) * slab]


def expert_kernel(count, total, ei_ref, *refs):
    x_refs, g_refs, p_refs = refs[:count], refs[count : 2 * count], refs[2 * count : 3 * count]
    gate_ref, wg_ref, wu_ref, wd_ref = refs[3 * count : 3 * count + 4]
    outs = refs[3 * count + 4 :]
    out_refs, back_refs, grads_ref = outs[:count], outs[count : 2 * count], outs[2 * count]
    capacity, width = x_refs[0].shape
    expert = ei_ref[0] * pl.num_programs(0) + pl.program_id(0)
    x = jnp.concatenate([r[...] for r in x_refs], axis=0)
    g = jnp.concatenate([r[...] for r in g_refs], axis=0)
    gate = jnp.concatenate(
        [
            jnp.sum(p_refs[s][...].astype(F32) * gate_ref[0, s : s + 1, :], axis=1, keepdims=True)
            for s in range(count)
        ],
        axis=0,
    )
    wg, wu, wd = wg_ref[0], wu_ref[0], wd_ref[0]
    gate_pre = dot(x, wg)
    up_pre = dot(x, wu)
    back_active = dot(g, wd)
    sig = 1.0 / (1.0 + jnp.exp(-gate_pre))
    silu = gate_pre * sig
    active = silu * up_pre
    slot_gate = RES_MULT * gate
    gate_grad = slot_gate * jnp.sum(active * back_active, axis=1, keepdims=True)
    active_low = (active * slot_gate).astype(BF)
    back_active = back_active * slot_gate
    gate_back = (back_active * up_pre * sig * (1.0 + gate_pre * (1.0 - sig))).astype(BF)
    up_back = (back_active * silu).astype(BF)
    out = dot(active_low, wd, 1, 1).astype(BF)
    back = (dot(gate_back, wg, 1, 1) + dot(up_back, wu, 1, 1)).astype(BF)
    lane = lax.broadcasted_iota(jnp.int32, (gate_grad.shape[0], PAD), 1)
    high = gate_grad.astype(BF).astype(F32)
    extra = jnp.where(
        lane == expert, high, jnp.where(lane == total + expert, gate_grad - high, 0.0)
    ).astype(BF)
    for s in range(count):
        rows = slice(s * capacity, (s + 1) * capacity)
        out_refs[s][...] = out[rows]
        back_refs[s][:, :width] = back[rows]
        back_refs[s][:, width:] = extra[rows]
    slabs, rows = grads_ref.shape[0], grads_ref.shape[3]
    for k, (a, b) in enumerate(((x, gate_back), (x, up_back), (g, active_low))):
        grads_ref[:, k, 0] = dot(a, b, 0, 0).astype(BF).reshape(slabs, rows, b.shape[1])


def run_experts(index, xs, gs, places, gates, wg, wu, wd, slabs, total):
    count = len(xs)
    experts, width, hidden = wg.shape
    capacity = xs[0].shape[0] // experts
    block = lambda w: pl.BlockSpec((capacity, w), lambda e, i: (e, 0))
    weight = pl.BlockSpec((1, width, hidden), lambda e, i: (e, 0, 0))
    rows = width // slabs
    flops = 2 * 9 * count * experts * capacity * width * hidden
    return pl.pallas_call(
        functools.partial(expert_kernel, count, total),
        grid_spec=pltpu.PrefetchScalarGridSpec(
            num_scalar_prefetch=1,
            grid=(experts,),
            in_specs=[block(width)] * (2 * count)
            + [block(places[0].shape[1])] * count
            + [pl.BlockSpec((1,) + gates.shape[1:], lambda e, i: (e, 0, 0))]
            + [weight] * 3,
            out_specs=[block(width)] * count
            + [block(width + PAD)] * count
            + [pl.BlockSpec((slabs, 3, 1, rows, hidden), lambda e, i: (0, 0, e, 0, 0))],
        ),
        out_shape=[jax.ShapeDtypeStruct((experts * capacity, width), BF)] * count
        + [jax.ShapeDtypeStruct((experts * capacity, width + PAD), BF)] * count
        + [jax.ShapeDtypeStruct((slabs, 3, experts, rows, hidden), BF)],
        compiler_params=pltpu.CompilerParams(
            dimension_semantics=("arbitrary",), vmem_limit_bytes=60 * 2**20
        ),
        cost_estimate=pl.CostEstimate(
            flops=flops,
            bytes_accessed=2 * (4 * count * experts * capacity * width + 6 * wg.size),
            transcendentals=count * experts * capacity * hidden,
        ),
        name="experts",
    )(index, *xs, *gs, *places, gates, wg, wu, wd)


def body(
    tokens,
    cotangent,
    norm_attn,
    norm_moe,
    w_query,
    w_key,
    w_value,
    w_out,
    w_router,
    w_gate,
    w_up,
    w_down,
    routes,
):
    local_rows, width = tokens.shape
    count = lax.axis_size("expert")
    slabs = lax.axis_size("dp")
    local_experts = w_gate.shape[1]
    expert_total = local_experts * count
    capacity = min(local_rows, max(2, local_rows * TOP * 7 // (4 * expert_total)))
    capacity = -(-capacity // 16) * 16
    query_width = w_query.shape[1]
    key_width = w_key.shape[1]
    qkv_width = query_width + 2 * key_width
    me = lax.axis_index("expert")

    pad = jnp.zeros((width // slabs, PAD - expert_total - 2), BF)
    packed = jnp.concatenate(
        [w_query, w_key, w_value, w_router, norm_attn[:, None], norm_moe[:, None], pad], axis=1
    )
    full = lax.all_gather(packed, "dp", axis=0, tiled=True)
    routes_low = jnp.concatenate(
        [routes.astype(BF), jnp.zeros((local_rows, PAD - TOP), BF)], axis=1
    )
    side_rows = jnp.concatenate([cotangent, routes_low], axis=1)
    sources = [lax.rem(me + count - s, count) for s in range(count)]
    key_pos = jnp.concatenate(
        [i * local_rows + jnp.arange(local_rows, dtype=jnp.int32) for i in sources]
    )
    cos, sin = rope_tables(key_pos)
    token_blocks, cot_down = [tokens], [side_rows]
    turned, weights = [], [w_gate, w_up, w_down]
    for step in range(1, count):
        up = upward(token_blocks[-1], "expert", count, 1, step - 1)
        down = downward(cot_down[-1], "expert", count, 1, step - 1)
        if weights:
            turned.append(jnp.transpose(weights.pop(0), (1, 0, 2)))
            up, down, turned, weights = lax.optimization_barrier((up, down, turned, weights))
        token_blocks.append(up)
        cot_down.append(down)
    wg, wu, wd = turned
    full, token_blocks, cot_down, w_out, cos, sin = lax.optimization_barrier(
        (full, token_blocks, cot_down, w_out, cos, sin)
    )
    out_full = lax.all_gather(w_out, "dp", axis=0, tiled=True)
    side_rows = cot_down[0]
    cot_up = [side_rows, upward(side_rows, "expert", count)]
    cot_up = cot_up + [upward(side_rows, "expert", count, s) for s in (2,) if count > 2]

    me_ref = jnp.stack([me, lax.axis_index("dp")]).astype(jnp.int32)
    normed_all, side, query, key, value, attended, lse = run_front(
        me_ref, token_blocks, full, cos, sin, query_width, key_width, expert_total
    )
    hidden = tokens.astype(F32)
    inverse_one = inverse_rms(hidden)
    gain_one = side[expert_total : expert_total + 1]
    gain_two = side[expert_total + 1 : expert_total + 2]
    router_full = full[:, qkv_width : qkv_width + expert_total]
    middle = hidden + RES_MULT * dot(attended, out_full)
    inverse_two = inverse_rms(middle)
    normed_two = (middle * inverse_two * gain_two).astype(BF)

    cot_up, cot_down, _ = lax.optimization_barrier((cot_up, cot_down, normed_two))
    while len(cot_up) < count:
        cot_up.append(upward(cot_up[-1], "expert", count, 1, len(cot_up) - 1))
    cot_blocks = [side_rows] + [cot_up[s] + cot_down[count - s] for s in range(1, count)]
    row = lax.broadcasted_iota(jnp.int32, (local_rows, local_rows), 0)
    col = lax.broadcasted_iota(jnp.int32, (local_rows, local_rows), 1)
    earlier = (row < col).astype(BF)
    all_ids = jnp.arange(expert_total, dtype=jnp.int32)
    own_ids = me * local_experts + jnp.arange(local_experts, dtype=jnp.int32)
    route_blocks, hots, hot_locals, places, cot_slots = [], [], [], [], []
    for s in range(count):
        named = cot_blocks[s][:, width : width + TOP].astype(F32).astype(jnp.int32)
        hot = jnp.any(named[:, :, None] == all_ids[None, None, :], axis=1)
        hot_local = jnp.any(
            named.T[None, :, :] == own_ids[:, None, None], axis=1
        )
        position = dot(hot_local.astype(BF), earlier).astype(jnp.int32)
        position = jnp.where(hot_local, position, -1)
        slots = jnp.arange(capacity, dtype=jnp.int32)
        place = (position[:, None, :] == slots[None, :, None]).astype(BF)
        place = place.reshape(local_experts * capacity, local_rows)
        hots.append(hot)
        hot_locals.append(hot_local)
        places.append(place)
        cot_slots.append(dot(place, cot_blocks[s][:, :width]).astype(BF))

    second_blocks = line_gather(normed_two, "expert", count)
    slot_rows, gates = [], []
    for s in range(count):
        logits = dot(second_blocks[s], router_full)
        masked = jnp.where(hots[s], logits, -1e30)
        exponent = jnp.where(
            hots[s], jnp.exp(masked - jnp.max(masked, axis=1, keepdims=True)), 0.0
        )
        gates.append(exponent / jnp.sum(exponent, axis=1, keepdims=True))
        slot_rows.append(dot(places[s], second_blocks[s]).astype(BF))
    gate_rows = jnp.stack(
        [lax.dynamic_slice_in_dim(g.T, me * local_experts, local_experts, 0) for g in gates],
        axis=1,
    )
    results = run_experts(
        me_ref,
        slot_rows,
        cot_slots,
        places,
        gate_rows,
        wg,
        wu,
        wd,
        slabs,
        expert_total,
    )
    slot_outs, slot_backs, expert_grads = (
        results[:count],
        results[count : 2 * count],
        results[2 * count],
    )
    back_sum = line_scatter(
        [dot(places[s], slot_backs[s], 0, 0).astype(BF) for s in range(count)], "expert", count
    )
    mix_parts = [dot(places[s], slot_outs[s], 0, 0).astype(BF) for s in range(count)]
    expert_owned = lax.psum_scatter(expert_grads, "dp", scatter_dimension=0, tiled=True)

    gate_own = gates[0]
    weighted = (
        back_sum[:, width : width + expert_total]
        + back_sum[:, width + expert_total : width + 2 * expert_total]
    )
    grad_logits = (weighted - gate_own * jnp.sum(weighted, axis=1, keepdims=True)).astype(BF)
    grad_normed_two = back_sum[:, :width] + dot(grad_logits, router_full, 1, 1)
    grad_gain_two = jnp.sum(grad_normed_two * middle * inverse_two, axis=0, keepdims=True)
    grad_middle = cotangent.astype(F32) + norm_back(middle, inverse_two, gain_two, grad_normed_two)
    branch_back = (RES_MULT * grad_middle).astype(BF)
    logits_wide = jnp.pad(grad_logits, ((0, 0), (0, PAD - expert_total)))
    out_keep, out_send = run_out(
        me_ref, attended, branch_back, normed_two, logits_wide, grad_gain_two, slabs, expert_total
    )
    out_state = trade(out_keep, out_send, 0, slabs)
    mix_parts, out_state, branch_back = lax.optimization_barrier(
        (mix_parts, out_state, branch_back)
    )
    near = send_near(mix_parts, "expert", count)
    out_stages = slab_stages(out_state, slabs)
    out_halves = next(out_stages)
    query_pre, key_pre, value_pre, *qkv_grads = run_back(
        me_ref, branch_back, out_full, query, key, value, lse, cos, sin, normed_all.T, slabs
    )
    qkv_grads, key_pre, value_pre, near, out_halves = lax.optimization_barrier(
        (qkv_grads, key_pre, value_pre, near, out_halves)
    )
    key_value_part = jnp.concatenate([key_pre, value_pre], axis=1)
    key_value_sum = [key_value_part[:local_rows]]
    key_value_came = [
        downward(key_value_part[s * local_rows : (s + 1) * local_rows], "expert", count, s)
        for s in range(1, count)
    ]
    qkv_state = trade(*qkv_grads, 0, slabs)
    qkv_state, came = lax.optimization_barrier((qkv_state, key_value_came[0]))
    key_value_sum.append(came)
    qkv_stages = slab_stages(qkv_state, slabs)
    qkv_halves = next(qkv_stages)
    for step in range(slabs.bit_length() - 3):
        out_halves = out_stages.send(out_halves)
        qkv_halves, out_halves, came = lax.optimization_barrier(
            (qkv_halves, out_halves, key_value_came[1 + step : 2 + step])
        )
        key_value_sum += came
        qkv_halves = qkv_stages.send(qkv_halves)
    left = key_value_came[len(key_value_sum) - 1 :]
    out_parts = own_parts(*out_halves, me, count)
    out_came = send_parts(out_parts, "expert", count)
    qkv_halves, left, out_came, far = lax.optimization_barrier(
        (qkv_halves, left, out_came, mix_parts[2:-1])
    )
    key_value_sum = add_up(key_value_sum + left).astype(BF)
    out_sum = add_up(out_parts[:1] + out_came)
    qkv_parts = own_parts(*qkv_halves, me, count)
    qkv_sum = add_up(qkv_parts[:1] + send_parts(qkv_parts, "expert", count))
    far = send_far(far, "expert", count)
    output = (middle + add_up(mix_parts[:1] + near + far)).astype(BF)
    pairs = key_width // PAIR
    qkv_sum = qkv_sum.reshape(qkv_sum.shape[0], pairs, (GROUP + 2) * PAIR)
    wide = GROUP * PAIR
    qkv_sum = jnp.concatenate(
        [
            part.reshape(qkv_sum.shape[0], -1)
            for part in (
                qkv_sum[:, :, :wide],
                qkv_sum[:, :, wide : wide + PAIR],
                qkv_sum[:, :, wide + PAIR :],
            )
        ],
        axis=1,
    )
    grad_normed_one = dot(query_pre, full[:, :query_width], 1, 1) + dot(
        key_value_sum, full[:, query_width:qkv_width], 1, 1
    )
    grad_tokens = (grad_middle + norm_back(hidden, inverse_one, gain_one, grad_normed_one)).astype(
        BF
    )
    own = qkv_sum.shape[0]
    own_packed = lax.dynamic_slice_in_dim(packed, me * own, own, 0).astype(F32)
    gain_one_sum = (
        jnp.sum(own_packed[:, :qkv_width] * qkv_sum, axis=1)
        / own_packed[:, qkv_width + expert_total]
    )
    owned = [jnp.transpose(expert_owned[0, k], (1, 0, 2)).astype(F32) for k in range(3)]
    return (
        output,
        grad_tokens,
        gain_one_sum,
        out_sum[:, width + expert_total],
        qkv_sum[:, :query_width],
        qkv_sum[:, query_width : query_width + key_width],
        qkv_sum[:, query_width + key_width :],
        out_sum[:, :width],
        out_sum[:, width : width + expert_total],
        *owned,
    )


def solution(mesh):
    rows = P(("dp", "expert"), None)
    in_specs = (
        [rows, rows, P("dp"), P("dp")]
        + [P("dp", None)] * 5
        + [P(None, "expert", None)] * 3
        + [rows]
    )
    out_specs = (
        [rows, rows, P(("dp", "expert")), P(("dp", "expert"))]
        + [rows] * 5
        + [P("dp", "expert", None)] * 3
    )
    return jax.shard_map(
        body, mesh=mesh, in_specs=tuple(in_specs), out_specs=tuple(out_specs), check_vma=False
    )
```

```python
import functools

import jax
import jax.numpy as jnp
from jax import lax
from jax.experimental import pallas as pl
from jax.experimental.pallas import tpu as pltpu
from jax.sharding import PartitionSpec as P

HEADS = 24
KV_HEADS = 8
HEAD_DIM = 64
TOP = 8
GROUP = HEADS // KV_HEADS
PAD = 128
PAIR = 2 * HEAD_DIM


RES_MULT = 0.22
ATT_MULT = 0.015625
NORM_EPS = 1e-06
ROPE_BASE = 10000.0
BF = jnp.bfloat16
F32 = jnp.float32


def dot(a, b, ca=1, cb=0):
    return lax.dot_general(a, b, (((ca,), (cb,)), ((), ())), preferred_element_type=F32)


def inverse_rms(hidden):
    return lax.rsqrt(jnp.mean(hidden * hidden, axis=-1, keepdims=True) + NORM_EPS)


def norm_back(hidden, inverse, gain_vector, grad_normed):
    weighted = grad_normed * gain_vector
    return inverse * weighted - hidden * inverse**3 * jnp.mean(
        weighted * hidden, axis=-1, keepdims=True
    )


def rope_tables(positions):
    half = HEAD_DIM // 2
    frequency = ROPE_BASE ** (-(jnp.arange(half, dtype=F32) * 2.0 / HEAD_DIM))
    angles = positions.astype(F32)[:, None] * frequency[None, :]
    cos, sin = jnp.cos(angles), jnp.sin(angles)
    return jnp.concatenate([cos] * 4, axis=1), jnp.concatenate([-sin, sin] * 2, axis=1)


def swap_halves(x):
    half = HEAD_DIM // 2
    lane = lax.broadcasted_iota(jnp.int32, x.shape, 1)
    return jnp.where(
        lane % HEAD_DIM < half, pltpu.roll(x, PAIR - half, 1), pltpu.roll(x, half, 1)
    )


def rope(x, cos, sin):
    return jnp.concatenate(
        [
            x[:, i : i + PAIR] * cos + swap_halves(x[:, i : i + PAIR]) * sin
            for i in range(0, x.shape[1], PAIR)
        ],
        axis=1,
    )


def causal_bias(me, count, rows):
    query = me * rows + lax.broadcasted_iota(jnp.int32, (rows, count * rows), 0)
    key = lax.broadcasted_iota(jnp.int32, (rows, count * rows), 1)
    source = me - key // rows
    source = jnp.where(source < 0, source + count, source)
    return jnp.where(source * rows + key % rows <= query, 0.0, -1e30)


def front_kernel(count, gain_at, me_ref, *refs):
    token_refs = refs[:count]
    wq_ref, wk_ref, wv_ref, side_ref, cos_ref, sin_ref = refs[count : count + 6]
    normed_ref, side_out, q_ref, k_ref, v_ref, att_ref, lse_ref, bias_ref = refs[count + 6 :]
    rows = token_refs[0].shape[0]

    @pl.when(pl.program_id(0) == 0)
    def _():
        side = side_ref[...].astype(F32).T
        side_out[...] = side
        for s in range(count):
            hidden = token_refs[s][...].astype(F32)
            normed = hidden * inverse_rms(hidden) * side[gain_at : gain_at + 1]
            normed_ref[s * rows : (s + 1) * rows] = normed.astype(BF)
        bias_ref[...] = causal_bias(me_ref[0], count, rows)

    cos, sin = cos_ref[...], sin_ref[...]
    query = rope(dot(normed_ref[:rows], wq_ref[...]), cos[:rows], sin[:rows]).astype(BF)
    query = query * ATT_MULT
    q_ref[...] = query
    both = dot(normed_ref[...], jnp.concatenate([wk_ref[...], wv_ref[...]], axis=1))
    key = rope(both[:, :PAIR], cos, sin).astype(BF)
    value = both[:, PAIR:].astype(BF)
    k_ref[...] = key
    v_ref[...] = value
    lse_ref[...] = jnp.zeros_like(lse_ref)
    for head in range(2 * GROUP):
        at = slice(head * HEAD_DIM, (head + 1) * HEAD_DIM)
        kv_at = slice(head // GROUP * HEAD_DIM, (head // GROUP + 1) * HEAD_DIM)
        scores = dot(query[:, at], key[:, kv_at], 1, 1) + bias_ref[...]
        peak = jnp.max(scores, axis=1, keepdims=True)
        weight = jnp.exp(scores - peak)
        total = jnp.sum(weight, axis=1, keepdims=True)
        probs = (weight * (1.0 / total)).astype(BF)
        att_ref[:, at] = dot(probs, value[:, kv_at]).astype(BF)
        lse_ref[:, head : head + 1] = peak + jnp.log(total)


def run_front(me, tokens, full, cos, sin, query_width, key_width, gain_at):
    count, (rows, width) = len(tokens), tokens[0].shape
    length, pairs, wide = count * rows, key_width // PAIR, GROUP * PAIR
    whole = lambda shape: pl.BlockSpec(shape, lambda p, i: (0, 0))
    column = lambda r, w, first: pl.BlockSpec((r, w), lambda p, i: (0, first + p))
    flops = 2 * width * (rows * query_width + 2 * length * key_width)
    flops += 4 * rows * length * query_width
    return pl.pallas_call(
        functools.partial(front_kernel, count, gain_at),
        grid_spec=pltpu.PrefetchScalarGridSpec(
            num_scalar_prefetch=1,
            grid=(pairs,),
            in_specs=[whole((rows, width))] * count
            + [
                column(width, wide, 0),
                column(width, PAIR, query_width // PAIR),
                column(width, PAIR, (query_width + key_width) // PAIR),
                pl.BlockSpec(
                    (width, PAIR), lambda p, i: (0, (query_width + 2 * key_width) // PAIR)
                ),
                whole((length, PAIR)),
                whole((length, PAIR)),
            ],
            out_specs=[
                whole((length, width)),
                whole((PAIR, width)),
                column(rows, wide, 0),
                column(length, PAIR, 0),
                column(length, PAIR, 0),
                column(rows, wide, 0),
                column(rows, PAIR, 0),
            ],
            scratch_shapes=[pltpu.VMEM((rows, length), F32)],
        ),
        out_shape=[
            jax.ShapeDtypeStruct((length, width), BF),
            jax.ShapeDtypeStruct((PAIR, width), F32),
            jax.ShapeDtypeStruct((rows, query_width), BF),
            jax.ShapeDtypeStruct((length, key_width), BF),
            jax.ShapeDtypeStruct((length, key_width), BF),
            jax.ShapeDtypeStruct((rows, query_width), BF),
            jax.ShapeDtypeStruct((rows, pairs * PAIR), F32),
        ],
        compiler_params=pltpu.CompilerParams(
            dimension_semantics=("arbitrary",), vmem_limit_bytes=56 * 2**20
        ),
        cost_estimate=pl.CostEstimate(
            flops=flops,
            bytes_accessed=4 * (length * width + full.size),
            transcendentals=rows * length * query_width // HEAD_DIM,
        ),
        name="front",
    )(me, *tokens, full, full, full, full, cos, sin)


def back_kernel(count, me_ref, *refs):
    branch_ref, wo_ref, q_ref, k_ref, v_ref, lse_ref, cos_ref, sin_ref, normed_ref = refs[:9]
    dq_ref, dk_ref, dv_ref, keep_ref, send_ref, bias_ref = refs[9:]
    rows = branch_ref.shape[0]

    @pl.when(pl.program_id(0) == 0)
    def _():
        bias_ref[...] = causal_bias(me_ref[0], count, rows)

    grad = dot(branch_ref[...], wo_ref[...], 1, 1).astype(BF)
    query, key, value = q_ref[...], k_ref[...], v_ref[...]
    dqs, dks, dvs = [], [], []
    for head in range(2 * GROUP):
        at = slice(head * HEAD_DIM, (head + 1) * HEAD_DIM)
        kv_at = slice(head // GROUP * HEAD_DIM, (head // GROUP + 1) * HEAD_DIM)
        scores = dot(query[:, at], key[:, kv_at], 1, 1) + bias_ref[...]
        probs = jnp.exp(scores - lse_ref[:, head : head + 1])
        probs_back = dot(grad[:, at], value[:, kv_at], 1, 1)
        delta = jnp.sum(probs * probs_back, axis=1, keepdims=True)
        scores_back = (probs * (probs_back - delta)).astype(BF)
        dqs.append(dot(scores_back, key[:, kv_at]) * ATT_MULT)
        dk = dot(scores_back, query[:, at], 0, 0)
        dv = dot(probs.astype(BF), grad[:, at], 0, 0)
        if head % GROUP == 0:
            dks.append(dk)
            dvs.append(dv)
        else:
            dks[-1] = dks[-1] + dk
            dvs[-1] = dvs[-1] + dv
    cos, sin = cos_ref[...], sin_ref[...]
    dq = rope(jnp.concatenate(dqs, axis=1), cos[:rows], -sin[:rows]).astype(BF)
    dk = rope(jnp.concatenate(dks, axis=1), cos, -sin).astype(BF)
    dv = jnp.concatenate(dvs, axis=1).astype(BF)
    dq_ref[...] = dq
    dk_ref[...] = dk
    dv_ref[...] = dv
    wide = dq.shape[1]
    grad_q = dot(normed_ref[:, :rows], dq).astype(BF)
    grad_kv = dot(normed_ref[...], jnp.concatenate([dk, dv], axis=1)).astype(BF)
    store_slabs(keep_ref, send_ref, me_ref[1], slice(0, wide), grad_q)
    store_slabs(keep_ref, send_ref, me_ref[1], slice(wide, wide + 2 * PAIR), grad_kv)


def out_kernel(total, me_ref, att_ref, branch_ref, normed_ref, logit_ref, gain_ref, *grad_refs):
    width = branch_ref.shape[1]
    router = dot(normed_ref[...].T, logit_ref[...])
    gain = jnp.broadcast_to(gain_ref[0:1], (PAD, width)).T
    lane = lax.broadcasted_iota(jnp.int32, (width, PAD), 1)
    side = jnp.where(lane == total, gain, router).astype(BF)
    main = dot(att_ref[...].T, branch_ref[...]).astype(BF)
    store_slabs(*grad_refs, me_ref[1], slice(0, width), main)
    store_slabs(*grad_refs, me_ref[1], slice(width, width + PAD), side)


def run_out(me, attended, branch, normed, logits, gain, slabs, total):
    rows, width = branch.shape
    inner = attended.shape[1]
    spec = pl.BlockSpec(memory_space=pltpu.VMEM)
    return pl.pallas_call(
        functools.partial(out_kernel, total),
        in_specs=[pl.BlockSpec(memory_space=pltpu.SMEM)] + [spec] * 5,
        out_specs=[spec] * 2,
        out_shape=[jax.ShapeDtypeStruct((slabs // 2, inner // slabs, width + PAD), BF)] * 2,
        compiler_params=pltpu.CompilerParams(vmem_limit_bytes=48 * 2**20),
        cost_estimate=pl.CostEstimate(
            flops=2 * rows * inner * (width + PAD),
            bytes_accessed=2 * (3 * rows * width + inner * (width + PAD)),
            transcendentals=0,
        ),
        name="out_grad",
    )(me, attended, branch, normed, logits, gain)


def run_back(me, branch, out_full, query, key, value, lse, cos, sin, normed_t, slabs):
    (rows, width), (length, key_width) = branch.shape, key.shape
    count, pairs, wide = length // rows, key_width // PAIR, GROUP * PAIR
    whole = lambda shape: pl.BlockSpec(shape, lambda p, i: (0, 0))
    column = lambda r, w: pl.BlockSpec((r, w), lambda p, i: (0, p))
    flops = 2 * width * (2 * rows * query.shape[1] + 2 * length * key_width)
    flops += 10 * rows * length * query.shape[1]
    return pl.pallas_call(
        functools.partial(back_kernel, count),
        grid_spec=pltpu.PrefetchScalarGridSpec(
            num_scalar_prefetch=1,
            grid=(pairs,),
            in_specs=[
                whole((rows, width)),
                pl.BlockSpec((wide, width), lambda p, i: (p, 0)),
                column(rows, wide),
                column(length, PAIR),
                column(length, PAIR),
                column(rows, PAIR),
                whole((length, PAIR)),
                whole((length, PAIR)),
                whole((width, length)),
            ],
            out_specs=[
                column(rows, wide),
                column(length, PAIR),
                column(length, PAIR),
            ]
            + [pl.BlockSpec((slabs // 2, width // slabs, wide + 2 * PAIR), lambda p, i: (0, 0, p))]
            * 2,
            scratch_shapes=[pltpu.VMEM((rows, length), F32)],
        ),
        out_shape=[
            jax.ShapeDtypeStruct(query.shape, BF),
            jax.ShapeDtypeStruct(key.shape, BF),
            jax.ShapeDtypeStruct(key.shape, BF),
        ]
        + [jax.ShapeDtypeStruct((slabs // 2, width // slabs, pairs * (wide + 2 * PAIR)), BF)] * 2,
        compiler_params=pltpu.CompilerParams(
            dimension_semantics=("arbitrary",), vmem_limit_bytes=56 * 2**20
        ),
        cost_estimate=pl.CostEstimate(
            flops=flops,
            bytes_accessed=2 * (length * width + 2 * width * query.shape[1]),
            transcendentals=rows * length * query.shape[1] // HEAD_DIM,
        ),
        name="back",
    )(me, branch, out_full, query, key, value, lse, cos, sin, normed_t)


def line_gather(block, axis, count):
    right, left = [block], [block]
    for step in range(1, count):
        right.append(
            lax.ppermute(right[-1], axis, [(i, i + 1) for i in range(step - 1, count - 1)])
        )
        left.append(lax.ppermute(left[-1], axis, [(i, i - 1) for i in range(1, count - step + 1)]))
    return [block] + [right[s] + left[count - s] for s in range(1, count)]


def line_scatter(parts, axis, count):
    if count == 1:
        return parts[0].astype(F32)
    right, left = parts[1], parts[count - 1]
    for step in range(1, count):
        right = lax.ppermute(right, axis, [(i, i + 1) for i in range(step)])
        left = lax.ppermute(left, axis, [(i, i - 1) for i in range(count - step, count)])
        if step < count - 1:
            right = parts[step + 1] + right
            left = parts[count - 1 - step] + left
    return parts[0].astype(F32) + right.astype(F32) + left.astype(F32)


def upward(block, axis, count, distance=1, first=0):
    pairs = [(i, i + distance) for i in range(first, count - distance)]
    return lax.ppermute(block, axis, pairs)


def downward(block, axis, count, distance=1, last=0):
    pairs = [(i, i - distance) for i in range(distance, count - last)]
    return lax.ppermute(block, axis, pairs)


def send_parts(parts, axis, count):
    return [
        lax.ppermute(parts[s], axis, [(i, (i + count - s) % count) for i in range(count)])
        for s in range(1, count)
    ]


def send_near(parts, axis, count):
    shifts = [s for s in {1: 1, count - 1: 1} if 0 < s < count]
    return [
        lax.ppermute(parts[s], axis, [(i, (i + count - s) % count) for i in range(count)])
        for s in shifts
    ]


def send_far(parts, axis, count):
    return [
        lax.ppermute(part, axis, [(i, (i + count - s) % count) for i in range(count)])
        for s, part in enumerate(parts, 2)
    ]


def add_up(parts):
    total = parts[0].astype(F32)
    for part in parts[1:]:
        total = total + part.astype(F32)
    return total


def trade(keep, send, bit, slabs):
    return keep + lax.ppermute(send, "dp", [(i, i ^ (1 << bit)) for i in range(slabs)])


def halve(x, bits, bit, slabs):
    at = bits.index(bit)
    keep, send = (lax.index_in_dim(x, i, at, False) for i in (0, 1))
    return trade(keep, send, bit, slabs), [b for b in bits if b != bit]


def slab_stages(x, slabs):
    top = slabs.bit_length() - 1
    bits = list(range(top - 1, 0, -1))
    x = x.reshape((2,) * (top - 1) + x.shape[1:])
    one, two = jnp.split(x, 2, axis=len(bits))
    bits_one, bits_two = bits, bits
    for k in range(len(bits)):
        one, bits_one = halve(one, bits_one, k + 1, slabs)
        two, bits_two = halve(two, bits_two, len(bits) - k, slabs)
        one, two = yield one, two


def own_parts(one, two, me, count):
    x = jnp.concatenate([one, two], axis=0)
    own = x.shape[0] // count
    return [
        lax.dynamic_slice_in_dim(x, lax.rem(me + count - s, count) * own, own, 0)
        for s in range(count)
    ]


def store_slabs(keep_ref, send_ref, own, at, value):
    half, slab, _ = keep_ref.shape
    for odd in (0, 1):

        @pl.when(lax.rem(own, 2) == odd)
        def _():
            for d in range(2 * half):
                ref = keep_ref if d % 2 == odd else send_ref
                place = lax.bitwise_xor(jnp.int32(d), own) // 2
                ref[place, :, at] = value[d * slab : (d + 1) * slab]


def expert_kernel(count, total, experts, first, me_ref, *refs):
    x_refs, g_refs, p_refs = refs[:count], refs[count : 2 * count], refs[2 * count : 3 * count]
    gate_ref, wg_ref, wu_ref, wd_ref = refs[3 * count : 3 * count + 4]
    outs = refs[-2 * count - 1 :]
    out_refs, back_refs, grads_ref = outs[:count], outs[count : 2 * count], outs[2 * count]
    capacity, width = x_refs[0].shape
    expert = me_ref[0] * experts + first + pl.program_id(0)
    x = jnp.concatenate([r[...] for r in x_refs], axis=0)
    g = jnp.concatenate([r[...] for r in g_refs], axis=0)
    gate = jnp.concatenate(
        [
            jnp.sum(p_refs[s][...].astype(F32) * gate_ref[0, s : s + 1, :], axis=1, keepdims=True)
            for s in range(count)
        ],
        axis=0,
    )
    wg, wu, wd = wg_ref[0], wu_ref[0], wd_ref[0]
    gate_pre = dot(x, wg)
    up_pre = dot(x, wu)
    back_active = dot(g, wd)
    sig = 1.0 / (1.0 + jnp.exp(-gate_pre))
    silu = gate_pre * sig
    active = silu * up_pre
    slot_gate = RES_MULT * gate
    gate_grad = slot_gate * jnp.sum(active * back_active, axis=1, keepdims=True)
    active_low = (active * slot_gate).astype(BF)
    back_active = back_active * slot_gate
    gate_back = (back_active * up_pre * sig * (1.0 + gate_pre * (1.0 - sig))).astype(BF)
    up_back = (back_active * silu).astype(BF)
    out = dot(active_low, wd, 1, 1).astype(BF)
    back = (dot(gate_back, wg, 1, 1) + dot(up_back, wu, 1, 1)).astype(BF)
    lane = lax.broadcasted_iota(jnp.int32, (gate_grad.shape[0], PAD), 1)
    high = gate_grad.astype(BF).astype(F32)
    extra = jnp.where(
        lane == expert, high, jnp.where(lane == total + expert, gate_grad - high, 0.0)
    ).astype(BF)
    for s in range(count):
        rows = slice(s * capacity, (s + 1) * capacity)
        out_refs[s][...] = out[rows]
        back_refs[s][:, :width] = back[rows]
        back_refs[s][:, width:] = extra[rows]
    slabs, rows = grads_ref.shape[0], grads_ref.shape[3]
    for k, (a, b) in enumerate(((x, gate_back), (x, up_back), (g, active_low))):
        grads_ref[:, k, 0] = dot(a, b, 0, 0).astype(BF).reshape(slabs, rows, b.shape[1])


def run_experts(index, xs, gs, places, gates, wg, wu, wd, slabs, total, first, number, earlier):
    count = len(xs)
    experts, width, hidden = wg.shape
    capacity = xs[0].shape[0] // experts
    block = lambda w: pl.BlockSpec((capacity, w), lambda e, i: (first + e, 0))
    weight = pl.BlockSpec((1, width, hidden), lambda e, i: (first + e, 0, 0))
    rows = width // slabs
    slots = count * number * capacity
    inputs = [*xs, *gs, *places, gates, wg, wu, wd, *earlier]
    return pl.pallas_call(
        functools.partial(expert_kernel, count, total, experts, first),
        grid_spec=pltpu.PrefetchScalarGridSpec(
            num_scalar_prefetch=1,
            grid=(number,),
            in_specs=[block(width)] * (2 * count)
            + [block(places[0].shape[1])] * count
            + [pl.BlockSpec((1,) + gates.shape[1:], lambda e, i: (first + e, 0, 0))]
            + [weight] * 3
            + [pl.BlockSpec(memory_space=pl.ANY)] * len(earlier),
            out_specs=[block(width)] * count
            + [block(width + PAD)] * count
            + [pl.BlockSpec((slabs, 3, 1, rows, hidden), lambda e, i: (0, 0, e, 0, 0))],
        ),
        out_shape=[jax.ShapeDtypeStruct((experts * capacity, width), BF)] * count
        + [jax.ShapeDtypeStruct((experts * capacity, width + PAD), BF)] * count
        + [jax.ShapeDtypeStruct((slabs, 3, number, rows, hidden), BF)],
        input_output_aliases={1 + len(inputs) - len(earlier) + i: i for i in range(len(earlier))},
        compiler_params=pltpu.CompilerParams(
            dimension_semantics=("arbitrary",), vmem_limit_bytes=60 * 2**20
        ),
        cost_estimate=pl.CostEstimate(
            flops=18 * slots * width * hidden,
            bytes_accessed=2 * (4 * slots * width + 6 * number * width * hidden),
            transcendentals=slots * hidden,
        ),
        name="experts",
    )(index, *inputs)


def owned_kernel(*refs):
    owned, sums = refs[-3:], refs[:-3]
    experts = sum(ref.shape[2] for ref in sums)
    at = 0
    for ref in sums:
        for e in range(ref.shape[2]):
            for k, out in enumerate(owned):
                out[pl.ds(at, ref.shape[3], stride=experts), :] = ref[0, k, e].astype(F32)
            at += 1


def run_owned(sums):
    rows, hidden = sums[0].shape[3:]
    experts = sum(x.shape[2] for x in sums)
    lanes = 128
    return pl.pallas_call(
        owned_kernel,
        grid=(hidden // lanes,),
        in_specs=[
            pl.BlockSpec((1, 3, x.shape[2], rows, lanes), lambda i: (0, 0, 0, 0, i)) for x in sums
        ],
        out_specs=[pl.BlockSpec((rows * experts, lanes), lambda i: (0, i))] * 3,
        out_shape=[jax.ShapeDtypeStruct((rows * experts, hidden), F32)] * 3,
        compiler_params=pltpu.CompilerParams(
            dimension_semantics=("arbitrary",), vmem_limit_bytes=32 * 2**20
        ),
        cost_estimate=pl.CostEstimate(
            flops=0, bytes_accessed=18 * rows * experts * hidden, transcendentals=0
        ),
        name="owned",
    )(*sums)


def body(
    tokens,
    cotangent,
    norm_attn,
    norm_moe,
    w_query,
    w_key,
    w_value,
    w_out,
    w_router,
    w_gate,
    w_up,
    w_down,
    routes,
):
    local_rows, width = tokens.shape
    count = lax.axis_size("expert")
    slabs = lax.axis_size("dp")
    local_experts = w_gate.shape[1]
    expert_total = local_experts * count
    capacity = min(local_rows, max(2, local_rows * TOP * 7 // (4 * expert_total)))
    capacity = -(-capacity // 16) * 16
    query_width = w_query.shape[1]
    key_width = w_key.shape[1]
    qkv_width = query_width + 2 * key_width
    me = lax.axis_index("expert")

    pad = jnp.zeros((width // slabs, PAD - expert_total - 2), BF)
    packed = jnp.concatenate(
        [w_query, w_key, w_value, w_router, norm_attn[:, None], norm_moe[:, None], pad], axis=1
    )
    full = lax.all_gather(packed, "dp", axis=0, tiled=True)
    routes_low = jnp.concatenate(
        [routes.astype(BF), jnp.zeros((local_rows, PAD - TOP), BF)], axis=1
    )
    side_rows = jnp.concatenate([cotangent, routes_low], axis=1)
    sources = [lax.rem(me + count - s, count) for s in range(count)]
    key_pos = jnp.concatenate(
        [i * local_rows + jnp.arange(local_rows, dtype=jnp.int32) for i in sources]
    )
    cos, sin = rope_tables(key_pos)
    token_blocks, cot_down = [tokens], [side_rows]
    turned, weights = [], [w_gate, w_up, w_down]
    for step in range(1, count):
        up = upward(token_blocks[-1], "expert", count, 1, step - 1)
        down = downward(cot_down[-1], "expert", count, 1, step - 1)
        if weights:
            turned.append(jnp.transpose(weights.pop(0), (1, 0, 2)))
            up, down, turned, weights = lax.optimization_barrier((up, down, turned, weights))
        token_blocks.append(up)
        cot_down.append(down)
    wg, wu, wd = turned
    full, token_blocks, cot_down, w_out, cos, sin = lax.optimization_barrier(
        (full, token_blocks, cot_down, w_out, cos, sin)
    )
    out_full = lax.all_gather(w_out, "dp", axis=0, tiled=True)
    side_rows = cot_down[0]
    cot_up = [side_rows, upward(side_rows, "expert", count)]
    cot_up = cot_up + [upward(side_rows, "expert", count, s) for s in (2,) if count > 2]

    me_ref = jnp.stack([me, lax.axis_index("dp")]).astype(jnp.int32)
    normed_all, side, query, key, value, attended, lse = run_front(
        me_ref, token_blocks, full, cos, sin, query_width, key_width, expert_total
    )
    hidden = tokens.astype(F32)
    inverse_one = inverse_rms(hidden)
    gain_one = side[expert_total : expert_total + 1]
    gain_two = side[expert_total + 1 : expert_total + 2]
    router_full = full[:, qkv_width : qkv_width + expert_total]
    middle = hidden + RES_MULT * dot(attended, out_full)
    inverse_two = inverse_rms(middle)
    normed_two = (middle * inverse_two * gain_two).astype(BF)

    cot_up, cot_down, _ = lax.optimization_barrier((cot_up, cot_down, normed_two))
    while len(cot_up) < count:
        cot_up.append(upward(cot_up[-1], "expert", count, 1, len(cot_up) - 1))
    cot_blocks = [side_rows] + [cot_up[s] + cot_down[count - s] for s in range(1, count)]
    row = lax.broadcasted_iota(jnp.int32, (local_rows, local_rows), 0)
    col = lax.broadcasted_iota(jnp.int32, (local_rows, local_rows), 1)
    earlier = (row < col).astype(BF)
    all_ids = jnp.arange(expert_total, dtype=jnp.int32)
    own_ids = me * local_experts + jnp.arange(local_experts, dtype=jnp.int32)
    route_blocks, hots, hot_locals, places, cot_slots = [], [], [], [], []
    for s in range(count):
        named = cot_blocks[s][:, width : width + TOP].astype(F32).astype(jnp.int32)
        hot = jnp.any(named[:, :, None] == all_ids[None, None, :], axis=1)
        hot_local = jnp.any(
            named.T[None, :, :] == own_ids[:, None, None], axis=1
        )
        position = dot(hot_local.astype(BF), earlier).astype(jnp.int32)
        position = jnp.where(hot_local, position, -1)
        slots = jnp.arange(capacity, dtype=jnp.int32)
        place = (position[:, None, :] == slots[None, :, None]).astype(BF)
        place = place.reshape(local_experts * capacity, local_rows)
        hots.append(hot)
        hot_locals.append(hot_local)
        places.append(place)
        cot_slots.append(dot(place, cot_blocks[s][:, :width]).astype(BF))

    second_blocks = line_gather(normed_two, "expert", count)
    slot_rows, gates = [], []
    for s in range(count):
        logits = dot(second_blocks[s], router_full)
        masked = jnp.where(hots[s], logits, -1e30)
        exponent = jnp.where(
            hots[s], jnp.exp(masked - jnp.max(masked, axis=1, keepdims=True)), 0.0
        )
        gates.append(exponent / jnp.sum(exponent, axis=1, keepdims=True))
        slot_rows.append(dot(places[s], second_blocks[s]).astype(BF))
    gate_rows = jnp.stack(
        [lax.dynamic_slice_in_dim(g.T, me * local_experts, local_experts, 0) for g in gates],
        axis=1,
    )
    early = max(1, local_experts // 4)
    results, expert_sums = [], []
    for first, number in ((0, early), (early, local_experts - early)):
        *results, grads = run_experts(
            me_ref,
            slot_rows,
            cot_slots,
            places,
            gate_rows,
            wg,
            wu,
            wd,
            slabs,
            expert_total,
            first,
            number,
            results,
        )
        expert_sums.append(lax.psum_scatter(grads, "dp", scatter_dimension=0, tiled=True))
    slot_outs, slot_backs = results[:count], results[count:]
    back_sum = line_scatter(
        [dot(places[s], slot_backs[s], 0, 0).astype(BF) for s in range(count)], "expert", count
    )
    mix_parts = [dot(places[s], slot_outs[s], 0, 0).astype(BF) for s in range(count)]

    gate_own = gates[0]
    weighted = (
        back_sum[:, width : width + expert_total]
        + back_sum[:, width + expert_total : width + 2 * expert_total]
    )
    grad_logits = (weighted - gate_own * jnp.sum(weighted, axis=1, keepdims=True)).astype(BF)
    grad_normed_two = back_sum[:, :width] + dot(grad_logits, router_full, 1, 1)
    grad_gain_two = jnp.sum(grad_normed_two * middle * inverse_two, axis=0, keepdims=True)
    grad_middle = cotangent.astype(F32) + norm_back(middle, inverse_two, gain_two, grad_normed_two)
    branch_back = (RES_MULT * grad_middle).astype(BF)
    logits_wide = jnp.pad(grad_logits, ((0, 0), (0, PAD - expert_total)))
    out_keep, out_send = run_out(
        me_ref, attended, branch_back, normed_two, logits_wide, grad_gain_two, slabs, expert_total
    )
    out_state = trade(out_keep, out_send, 0, slabs)
    mix_parts, out_state, branch_back = lax.optimization_barrier(
        (mix_parts, out_state, branch_back)
    )
    near = send_near(mix_parts, "expert", count)
    out_stages = slab_stages(out_state, slabs)
    out_halves = next(out_stages)
    query_pre, key_pre, value_pre, *qkv_grads = run_back(
        me_ref, branch_back, out_full, query, key, value, lse, cos, sin, normed_all.T, slabs
    )
    qkv_grads, key_pre, value_pre, near, out_halves = lax.optimization_barrier(
        (qkv_grads, key_pre, value_pre, near, out_halves)
    )
    key_value_part = jnp.concatenate([key_pre, value_pre], axis=1)
    key_value_sum = [key_value_part[:local_rows]]
    key_value_came = [
        downward(key_value_part[s * local_rows : (s + 1) * local_rows], "expert", count, s)
        for s in range(1, count)
    ]
    qkv_state = trade(*qkv_grads, 0, slabs)
    qkv_state, came = lax.optimization_barrier((qkv_state, key_value_came[0]))
    key_value_sum.append(came)
    qkv_stages = slab_stages(qkv_state, slabs)
    qkv_halves = next(qkv_stages)
    far, _ = lax.optimization_barrier((mix_parts[2:-1], qkv_state))
    far = send_far(far, "expert", count)
    for step in range(slabs.bit_length() - 3):
        out_halves = out_stages.send(out_halves)
        qkv_halves, out_halves, far, came = lax.optimization_barrier(
            (qkv_halves, out_halves, far, key_value_came[1 + step : 2 + step])
        )
        key_value_sum += came
        qkv_halves = qkv_stages.send(qkv_halves)
    left = key_value_came[len(key_value_sum) - 1 :]
    out_parts = own_parts(*out_halves, me, count)
    out_came = send_parts(out_parts, "expert", count)
    qkv_halves, left, out_came = lax.optimization_barrier((qkv_halves, left, out_came))
    key_value_sum = add_up(key_value_sum + left).astype(BF)
    out_sum = add_up(out_parts[:1] + out_came)
    qkv_parts = own_parts(*qkv_halves, me, count)
    qkv_sum = add_up(qkv_parts[:1] + send_parts(qkv_parts, "expert", count))
    output = (middle + add_up(mix_parts[:1] + near + far)).astype(BF)
    pairs = key_width // PAIR
    qkv_sum = qkv_sum.reshape(qkv_sum.shape[0], pairs, (GROUP + 2) * PAIR)
    wide = GROUP * PAIR
    qkv_sum = jnp.concatenate(
        [
            part.reshape(qkv_sum.shape[0], -1)
            for part in (
                qkv_sum[:, :, :wide],
                qkv_sum[:, :, wide : wide + PAIR],
                qkv_sum[:, :, wide + PAIR :],
            )
        ],
        axis=1,
    )
    grad_normed_one = dot(query_pre, full[:, :query_width], 1, 1) + dot(
        key_value_sum, full[:, query_width:qkv_width], 1, 1
    )
    grad_tokens = (grad_middle + norm_back(hidden, inverse_one, gain_one, grad_normed_one)).astype(
        BF
    )
    own = qkv_sum.shape[0]
    own_packed = lax.dynamic_slice_in_dim(packed, me * own, own, 0).astype(F32)
    gain_one_sum = (
        jnp.sum(own_packed[:, :qkv_width] * qkv_sum, axis=1)
        / own_packed[:, qkv_width + expert_total]
    )
    owned = [
        x.reshape(width // slabs, local_experts, x.shape[1]) for x in run_owned(expert_sums)
    ]
    return (
        output,
        grad_tokens,
        gain_one_sum,
        out_sum[:, width + expert_total],
        qkv_sum[:, :query_width],
        qkv_sum[:, query_width : query_width + key_width],
        qkv_sum[:, query_width + key_width :],
        out_sum[:, :width],
        out_sum[:, width : width + expert_total],
        *owned,
    )


def solution(mesh):
    rows = P(("dp", "expert"), None)
    in_specs = (
        [rows, rows, P("dp"), P("dp")]
        + [P("dp", None)] * 5
        + [P(None, "expert", None)] * 3
        + [rows]
    )
    out_specs = (
        [rows, rows, P(("dp", "expert")), P(("dp", "expert"))]
        + [rows] * 5
        + [P("dp", "expert", None)] * 3
    )
    return jax.shard_map(
        body, mesh=mesh, in_specs=tuple(in_specs), out_specs=tuple(out_specs), check_vma=False
    )
```

```python
import functools

import jax
import jax.numpy as jnp
from jax import lax
from jax.experimental import pallas as pl
from jax.experimental.pallas import tpu as pltpu
from jax.sharding import PartitionSpec as P

HEADS = 24
KV_HEADS = 8
HEAD_DIM = 64
TOP = 8
GROUP = HEADS // KV_HEADS
PAD = 128
PAIR = 2 * HEAD_DIM


RES_MULT = 0.22
ATT_MULT = 0.015625
NORM_EPS = 1e-06
ROPE_BASE = 10000.0
BF = jnp.bfloat16
F32 = jnp.float32


def dot(a, b, ca=1, cb=0):
    return lax.dot_general(a, b, (((ca,), (cb,)), ((), ())), preferred_element_type=F32)


def inverse_rms(hidden):
    return lax.rsqrt(jnp.mean(hidden * hidden, axis=-1, keepdims=True) + NORM_EPS)


def norm_back(hidden, inverse, gain_vector, grad_normed):
    weighted = grad_normed * gain_vector
    return inverse * weighted - hidden * inverse**3 * jnp.mean(
        weighted * hidden, axis=-1, keepdims=True
    )


def rope_tables(positions):
    half = HEAD_DIM // 2
    frequency = ROPE_BASE ** (-(jnp.arange(half, dtype=F32) * 2.0 / HEAD_DIM))
    angles = positions.astype(F32)[:, None] * frequency[None, :]
    cos, sin = jnp.cos(angles), jnp.sin(angles)
    return jnp.concatenate([cos] * 4, axis=1), jnp.concatenate([-sin, sin] * 2, axis=1)


def swap_halves(x):
    half = HEAD_DIM // 2
    lane = lax.broadcasted_iota(jnp.int32, x.shape, 1)
    return jnp.where(
        lane % HEAD_DIM < half, pltpu.roll(x, PAIR - half, 1), pltpu.roll(x, half, 1)
    )


def rope(x, cos, sin):
    return jnp.concatenate(
        [
            x[:, i : i + PAIR] * cos + swap_halves(x[:, i : i + PAIR]) * sin
            for i in range(0, x.shape[1], PAIR)
        ],
        axis=1,
    )


def causal_bias(me, count, rows):
    query = me * rows + lax.broadcasted_iota(jnp.int32, (rows, count * rows), 0)
    key = lax.broadcasted_iota(jnp.int32, (rows, count * rows), 1)
    source = me - key // rows
    source = jnp.where(source < 0, source + count, source)
    return jnp.where(source * rows + key % rows <= query, 0.0, -1e30)


def front_kernel(count, gain_at, me_ref, *refs):
    token_refs = refs[:count]
    wq_ref, wk_ref, wv_ref, side_ref, cos_ref, sin_ref = refs[count : count + 6]
    normed_ref, side_out, q_ref, k_ref, v_ref, att_ref, lse_ref, bias_ref = refs[count + 6 :]
    rows = token_refs[0].shape[0]

    @pl.when(pl.program_id(0) == 0)
    def _():
        side = side_ref[...].astype(F32).T
        side_out[...] = side
        for s in range(count):
            hidden = token_refs[s][...].astype(F32)
            normed = hidden * inverse_rms(hidden) * side[gain_at : gain_at + 1]
            normed_ref[s * rows : (s + 1) * rows] = normed.astype(BF)
        bias_ref[...] = causal_bias(me_ref[0], count, rows)

    cos, sin = cos_ref[...], sin_ref[...]
    query = rope(dot(normed_ref[:rows], wq_ref[...]), cos[:rows], sin[:rows]).astype(BF)
    query = query * ATT_MULT
    q_ref[...] = query
    both = dot(normed_ref[...], jnp.concatenate([wk_ref[...], wv_ref[...]], axis=1))
    key = rope(both[:, :PAIR], cos, sin).astype(BF)
    value = both[:, PAIR:].astype(BF)
    k_ref[...] = key
    v_ref[...] = value
    lse_ref[...] = jnp.zeros_like(lse_ref)
    for head in range(2 * GROUP):
        at = slice(head * HEAD_DIM, (head + 1) * HEAD_DIM)
        kv_at = slice(head // GROUP * HEAD_DIM, (head // GROUP + 1) * HEAD_DIM)
        scores = dot(query[:, at], key[:, kv_at], 1, 1) + bias_ref[...]
        peak = jnp.max(scores, axis=1, keepdims=True)
        weight = jnp.exp(scores - peak)
        total = jnp.sum(weight, axis=1, keepdims=True)
        probs = (weight * (1.0 / total)).astype(BF)
        att_ref[:, at] = dot(probs, value[:, kv_at]).astype(BF)
        lse_ref[:, head : head + 1] = peak + jnp.log(total)


def run_front(me, tokens, full, cos, sin, query_width, key_width, gain_at):
    count, (rows, width) = len(tokens), tokens[0].shape
    length, pairs, wide = count * rows, key_width // PAIR, GROUP * PAIR
    whole = lambda shape: pl.BlockSpec(shape, lambda p, i: (0, 0))
    column = lambda r, w, first: pl.BlockSpec((r, w), lambda p, i: (0, first + p))
    flops = 2 * width * (rows * query_width + 2 * length * key_width)
    flops += 4 * rows * length * query_width
    return pl.pallas_call(
        functools.partial(front_kernel, count, gain_at),
        grid_spec=pltpu.PrefetchScalarGridSpec(
            num_scalar_prefetch=1,
            grid=(pairs,),
            in_specs=[whole((rows, width))] * count
            + [
                column(width, wide, 0),
                column(width, PAIR, query_width // PAIR),
                column(width, PAIR, (query_width + key_width) // PAIR),
                pl.BlockSpec(
                    (width, PAIR), lambda p, i: (0, (query_width + 2 * key_width) // PAIR)
                ),
                whole((length, PAIR)),
                whole((length, PAIR)),
            ],
            out_specs=[
                whole((length, width)),
                whole((PAIR, width)),
                column(rows, wide, 0),
                column(length, PAIR, 0),
                column(length, PAIR, 0),
                column(rows, wide, 0),
                column(rows, PAIR, 0),
            ],
            scratch_shapes=[pltpu.VMEM((rows, length), F32)],
        ),
        out_shape=[
            jax.ShapeDtypeStruct((length, width), BF),
            jax.ShapeDtypeStruct((PAIR, width), F32),
            jax.ShapeDtypeStruct((rows, query_width), BF),
            jax.ShapeDtypeStruct((length, key_width), BF),
            jax.ShapeDtypeStruct((length, key_width), BF),
            jax.ShapeDtypeStruct((rows, query_width), BF),
            jax.ShapeDtypeStruct((rows, pairs * PAIR), F32),
        ],
        compiler_params=pltpu.CompilerParams(
            dimension_semantics=("arbitrary",), vmem_limit_bytes=56 * 2**20
        ),
        cost_estimate=pl.CostEstimate(
            flops=flops,
            bytes_accessed=4 * (length * width + full.size),
            transcendentals=rows * length * query_width // HEAD_DIM,
        ),
        name="front",
    )(me, *tokens, full, full, full, full, cos, sin)


def back_kernel(count, me_ref, *refs):
    branch_ref, wo_ref, q_ref, k_ref, v_ref, lse_ref, cos_ref, sin_ref, normed_ref = refs[:9]
    dq_ref, dk_ref, dv_ref, keep_ref, send_ref, bias_ref = refs[9:]
    rows = branch_ref.shape[0]

    @pl.when(pl.program_id(0) == 0)
    def _():
        bias_ref[...] = causal_bias(me_ref[0], count, rows)

    grad = dot(branch_ref[...], wo_ref[...], 1, 1).astype(BF)
    query, key, value = q_ref[...], k_ref[...], v_ref[...]
    dqs, dks, dvs = [], [], []
    for head in range(2 * GROUP):
        at = slice(head * HEAD_DIM, (head + 1) * HEAD_DIM)
        kv_at = slice(head // GROUP * HEAD_DIM, (head // GROUP + 1) * HEAD_DIM)
        scores = dot(query[:, at], key[:, kv_at], 1, 1) + bias_ref[...]
        probs = jnp.exp(scores - lse_ref[:, head : head + 1])
        probs_back = dot(grad[:, at], value[:, kv_at], 1, 1)
        delta = jnp.sum(probs * probs_back, axis=1, keepdims=True)
        scores_back = (probs * (probs_back - delta)).astype(BF)
        dqs.append(dot(scores_back, key[:, kv_at]) * ATT_MULT)
        dk = dot(scores_back, query[:, at], 0, 0)
        dv = dot(probs.astype(BF), grad[:, at], 0, 0)
        if head % GROUP == 0:
            dks.append(dk)
            dvs.append(dv)
        else:
            dks[-1] = dks[-1] + dk
            dvs[-1] = dvs[-1] + dv
    cos, sin = cos_ref[...], sin_ref[...]
    dq = rope(jnp.concatenate(dqs, axis=1), cos[:rows], -sin[:rows]).astype(BF)
    dk = rope(jnp.concatenate(dks, axis=1), cos, -sin).astype(BF)
    dv = jnp.concatenate(dvs, axis=1).astype(BF)
    dq_ref[...] = dq
    dk_ref[...] = dk
    dv_ref[...] = dv
    wide = dq.shape[1]
    grad_q = dot(normed_ref[:, :rows], dq).astype(BF)
    grad_kv = dot(normed_ref[...], jnp.concatenate([dk, dv], axis=1)).astype(BF)
    store_slabs(keep_ref, send_ref, me_ref[1], slice(0, wide), grad_q)
    store_slabs(keep_ref, send_ref, me_ref[1], slice(wide, wide + 2 * PAIR), grad_kv)


def out_kernel(total, me_ref, att_ref, branch_ref, normed_ref, logit_ref, gain_ref, *grad_refs):
    width = branch_ref.shape[1]
    router = dot(normed_ref[...].T, logit_ref[...])
    gain = jnp.broadcast_to(gain_ref[0:1], (PAD, width)).T
    lane = lax.broadcasted_iota(jnp.int32, (width, PAD), 1)
    side = jnp.where(lane == total, gain, router).astype(BF)
    main = dot(att_ref[...].T, branch_ref[...]).astype(BF)
    store_slabs(*grad_refs, me_ref[1], slice(0, width), main)
    store_slabs(*grad_refs, me_ref[1], slice(width, width + PAD), side)


def run_out(me, attended, branch, normed, logits, gain, slabs, total):
    rows, width = branch.shape
    inner = attended.shape[1]
    spec = pl.BlockSpec(memory_space=pltpu.VMEM)
    return pl.pallas_call(
        functools.partial(out_kernel, total),
        in_specs=[pl.BlockSpec(memory_space=pltpu.SMEM)] + [spec] * 5,
        out_specs=[spec] * 2,
        out_shape=[jax.ShapeDtypeStruct((slabs // 2, inner // slabs, width + PAD), BF)] * 2,
        compiler_params=pltpu.CompilerParams(vmem_limit_bytes=48 * 2**20),
        cost_estimate=pl.CostEstimate(
            flops=2 * rows * inner * (width + PAD),
            bytes_accessed=2 * (3 * rows * width + inner * (width + PAD)),
            transcendentals=0,
        ),
        name="out_grad",
    )(me, attended, branch, normed, logits, gain)


def run_back(me, branch, out_full, query, key, value, lse, cos, sin, normed_t, slabs):
    (rows, width), (length, key_width) = branch.shape, key.shape
    count, pairs, wide = length // rows, key_width // PAIR, GROUP * PAIR
    whole = lambda shape: pl.BlockSpec(shape, lambda p, i: (0, 0))
    column = lambda r, w: pl.BlockSpec((r, w), lambda p, i: (0, p))
    flops = 2 * width * (2 * rows * query.shape[1] + 2 * length * key_width)
    flops += 10 * rows * length * query.shape[1]
    return pl.pallas_call(
        functools.partial(back_kernel, count),
        grid_spec=pltpu.PrefetchScalarGridSpec(
            num_scalar_prefetch=1,
            grid=(pairs,),
            in_specs=[
                whole((rows, width)),
                pl.BlockSpec((wide, width), lambda p, i: (p, 0)),
                column(rows, wide),
                column(length, PAIR),
                column(length, PAIR),
                column(rows, PAIR),
                whole((length, PAIR)),
                whole((length, PAIR)),
                whole((width, length)),
            ],
            out_specs=[
                column(rows, wide),
                column(length, PAIR),
                column(length, PAIR),
            ]
            + [pl.BlockSpec((slabs // 2, width // slabs, wide + 2 * PAIR), lambda p, i: (0, 0, p))]
            * 2,
            scratch_shapes=[pltpu.VMEM((rows, length), F32)],
        ),
        out_shape=[
            jax.ShapeDtypeStruct(query.shape, BF),
            jax.ShapeDtypeStruct(key.shape, BF),
            jax.ShapeDtypeStruct(key.shape, BF),
        ]
        + [jax.ShapeDtypeStruct((slabs // 2, width // slabs, pairs * (wide + 2 * PAIR)), BF)] * 2,
        compiler_params=pltpu.CompilerParams(
            dimension_semantics=("arbitrary",), vmem_limit_bytes=56 * 2**20
        ),
        cost_estimate=pl.CostEstimate(
            flops=flops,
            bytes_accessed=2 * (length * width + 2 * width * query.shape[1]),
            transcendentals=rows * length * query.shape[1] // HEAD_DIM,
        ),
        name="back",
    )(me, branch, out_full, query, key, value, lse, cos, sin, normed_t)


def line_gather(block, axis, count):
    right, left = [block], [block]
    for step in range(1, count):
        right.append(
            lax.ppermute(right[-1], axis, [(i, i + 1) for i in range(step - 1, count - 1)])
        )
        left.append(lax.ppermute(left[-1], axis, [(i, i - 1) for i in range(1, count - step + 1)]))
    return [block] + [right[s] + left[count - s] for s in range(1, count)]


def line_scatter(parts, axis, count, beside):
    if count == 1:
        return parts[0].astype(F32), beside
    right, left, ready = parts[1], parts[count - 1], []
    for step in range(1, count):
        right = lax.ppermute(right, axis, [(i, i + 1) for i in range(step)])
        left = lax.ppermute(left, axis, [(i, i - 1) for i in range(count - step, count)])
        if beside:
            right, left, now = lax.optimization_barrier((right, left, beside.pop(0)))
            ready.append(now)
        if step < count - 1:
            right = parts[step + 1] + right
            left = parts[count - 1 - step] + left
    return parts[0].astype(F32) + right.astype(F32) + left.astype(F32), ready + beside


def upward(block, axis, count, distance=1, first=0):
    pairs = [(i, i + distance) for i in range(first, count - distance)]
    return lax.ppermute(block, axis, pairs)


def downward(block, axis, count, distance=1, last=0):
    pairs = [(i, i - distance) for i in range(distance, count - last)]
    return lax.ppermute(block, axis, pairs)


def send_parts(parts, axis, count):
    return [
        lax.ppermute(parts[s], axis, [(i, (i + count - s) % count) for i in range(count)])
        for s in range(1, count)
    ]


def send_near(parts, axis, count):
    shifts = [s for s in {1: 1, count - 1: 1} if 0 < s < count]
    return [
        lax.ppermute(parts[s], axis, [(i, (i + count - s) % count) for i in range(count)])
        for s in shifts
    ]


def send_far(parts, axis, count):
    return [
        lax.ppermute(part, axis, [(i, (i + count - s) % count) for i in range(count)])
        for s, part in enumerate(parts, 2)
    ]


def add_up(parts):
    total = parts[0].astype(F32)
    for part in parts[1:]:
        total = total + part.astype(F32)
    return total


def trade(keep, send, bit, slabs):
    return keep + lax.ppermute(send, "dp", [(i, i ^ (1 << bit)) for i in range(slabs)])


def halve(x, bits, bit, slabs):
    at = bits.index(bit)
    keep, send = (lax.index_in_dim(x, i, at, False) for i in (0, 1))
    return trade(keep, send, bit, slabs), [b for b in bits if b != bit]


def slab_stages(x, slabs):
    top = slabs.bit_length() - 1
    bits = list(range(top - 1, 0, -1))
    x = x.reshape((2,) * (top - 1) + x.shape[1:])
    one, two = jnp.split(x, 2, axis=len(bits))
    bits_one, bits_two = bits, bits
    for k in range(len(bits)):
        one, bits_one = halve(one, bits_one, k + 1, slabs)
        two, bits_two = halve(two, bits_two, len(bits) - k, slabs)
        one, two = yield one, two


def own_parts(one, two, me, count):
    x = jnp.concatenate([one, two], axis=0)
    own = x.shape[0] // count
    return [
        lax.dynamic_slice_in_dim(x, lax.rem(me + count - s, count) * own, own, 0)
        for s in range(count)
    ]


def store_slabs(keep_ref, send_ref, own, at, value):
    half, slab, _ = keep_ref.shape
    for odd in (0, 1):

        @pl.when(lax.rem(own, 2) == odd)
        def _():
            for d in range(2 * half):
                ref = keep_ref if d % 2 == odd else send_ref
                place = lax.bitwise_xor(jnp.int32(d), own) // 2
                ref[place, :, at] = value[d * slab : (d + 1) * slab]


def expert_kernel(count, total, experts, first, me_ref, *refs):
    x_refs, g_refs, p_refs = refs[:count], refs[count : 2 * count], refs[2 * count : 3 * count]
    gate_ref, wg_ref, wu_ref, wd_ref = refs[3 * count : 3 * count + 4]
    outs = refs[-2 * count - 1 :]
    out_refs, back_refs, grads_ref = outs[:count], outs[count : 2 * count], outs[2 * count]
    capacity, width = x_refs[0].shape
    expert = me_ref[0] * experts + first + pl.program_id(0)
    x = jnp.concatenate([r[...] for r in x_refs], axis=0)
    g = jnp.concatenate([r[...] for r in g_refs], axis=0)
    gate = jnp.concatenate(
        [
            jnp.sum(p_refs[s][...].astype(F32) * gate_ref[0, s : s + 1, :], axis=1, keepdims=True)
            for s in range(count)
        ],
        axis=0,
    )
    wg, wu, wd = wg_ref[0], wu_ref[0], wd_ref[0]
    gate_pre = dot(x, wg)
    up_pre = dot(x, wu)
    back_active = dot(g, wd)
    sig = 1.0 / (1.0 + jnp.exp(-gate_pre))
    silu = gate_pre * sig
    active = silu * up_pre
    slot_gate = RES_MULT * gate
    gate_grad = slot_gate * jnp.sum(active * back_active, axis=1, keepdims=True)
    active_low = (active * slot_gate).astype(BF)
    back_active = back_active * slot_gate
    gate_back = (back_active * up_pre * sig * (1.0 + gate_pre * (1.0 - sig))).astype(BF)
    up_back = (back_active * silu).astype(BF)
    out = dot(active_low, wd, 1, 1).astype(BF)
    back = (dot(gate_back, wg, 1, 1) + dot(up_back, wu, 1, 1)).astype(BF)
    lane = lax.broadcasted_iota(jnp.int32, (gate_grad.shape[0], PAD), 1)
    high = gate_grad.astype(BF).astype(F32)
    extra = jnp.where(
        lane == expert, high, jnp.where(lane == total + expert, gate_grad - high, 0.0)
    ).astype(BF)
    for s in range(count):
        rows = slice(s * capacity, (s + 1) * capacity)
        out_refs[s][...] = out[rows]
        back_refs[s][:, :width] = back[rows]
        back_refs[s][:, width:] = extra[rows]
    slabs, rows = grads_ref.shape[0], grads_ref.shape[3]
    for k, (a, b) in enumerate(((x, gate_back), (x, up_back), (g, active_low))):
        grads_ref[:, k, 0] = dot(a, b, 0, 0).astype(BF).reshape(slabs, rows, b.shape[1])


def run_experts(index, xs, gs, places, gates, wg, wu, wd, slabs, total, first, number, earlier):
    count = len(xs)
    experts, width, hidden = wg.shape
    capacity = xs[0].shape[0] // experts
    block = lambda w: pl.BlockSpec((capacity, w), lambda e, i: (first + e, 0))
    weight = pl.BlockSpec((1, width, hidden), lambda e, i: (first + e, 0, 0))
    rows = width // slabs
    slots = count * number * capacity
    inputs = [*xs, *gs, *places, gates, wg, wu, wd, *earlier]
    return pl.pallas_call(
        functools.partial(expert_kernel, count, total, experts, first),
        grid_spec=pltpu.PrefetchScalarGridSpec(
            num_scalar_prefetch=1,
            grid=(number,),
            in_specs=[block(width)] * (2 * count)
            + [block(places[0].shape[1])] * count
            + [pl.BlockSpec((1,) + gates.shape[1:], lambda e, i: (first + e, 0, 0))]
            + [weight] * 3
            + [pl.BlockSpec(memory_space=pl.ANY)] * len(earlier),
            out_specs=[block(width)] * count
            + [block(width + PAD)] * count
            + [pl.BlockSpec((slabs, 3, 1, rows, hidden), lambda e, i: (0, 0, e, 0, 0))],
        ),
        out_shape=[jax.ShapeDtypeStruct((experts * capacity, width), BF)] * count
        + [jax.ShapeDtypeStruct((experts * capacity, width + PAD), BF)] * count
        + [jax.ShapeDtypeStruct((slabs, 3, number, rows, hidden), BF)],
        input_output_aliases={1 + len(inputs) - len(earlier) + i: i for i in range(len(earlier))},
        compiler_params=pltpu.CompilerParams(
            dimension_semantics=("arbitrary",), vmem_limit_bytes=60 * 2**20
        ),
        cost_estimate=pl.CostEstimate(
            flops=18 * slots * width * hidden,
            bytes_accessed=2 * (4 * slots * width + 6 * number * width * hidden),
            transcendentals=slots * hidden,
        ),
        name="experts",
    )(index, *inputs)


def owned_kernel(*refs):
    owned, sums = refs[-3:], refs[:-3]
    experts = sum(ref.shape[2] for ref in sums)
    at = 0
    for ref in sums:
        for e in range(ref.shape[2]):
            for k, out in enumerate(owned):
                out[pl.ds(at, ref.shape[3], stride=experts), :] = ref[0, k, e].astype(F32)
            at += 1


def run_owned(sums):
    rows, hidden = sums[0].shape[3:]
    experts = sum(x.shape[2] for x in sums)
    lanes = 128
    return pl.pallas_call(
        owned_kernel,
        grid=(hidden // lanes,),
        in_specs=[
            pl.BlockSpec((1, 3, x.shape[2], rows, lanes), lambda i: (0, 0, 0, 0, i)) for x in sums
        ],
        out_specs=[pl.BlockSpec((rows * experts, lanes), lambda i: (0, i))] * 3,
        out_shape=[jax.ShapeDtypeStruct((rows * experts, hidden), F32)] * 3,
        compiler_params=pltpu.CompilerParams(
            dimension_semantics=("arbitrary",), vmem_limit_bytes=32 * 2**20
        ),
        cost_estimate=pl.CostEstimate(
            flops=0, bytes_accessed=18 * rows * experts * hidden, transcendentals=0
        ),
        name="owned",
    )(*sums)


def body(
    tokens,
    cotangent,
    norm_attn,
    norm_moe,
    w_query,
    w_key,
    w_value,
    w_out,
    w_router,
    w_gate,
    w_up,
    w_down,
    routes,
):
    local_rows, width = tokens.shape
    count = lax.axis_size("expert")
    slabs = lax.axis_size("dp")
    local_experts = w_gate.shape[1]
    expert_total = local_experts * count
    capacity = min(local_rows, max(2, local_rows * TOP * 7 // (4 * expert_total)))
    capacity = -(-capacity // 16) * 16
    query_width = w_query.shape[1]
    key_width = w_key.shape[1]
    qkv_width = query_width + 2 * key_width
    me = lax.axis_index("expert")

    pad = jnp.zeros((width // slabs, PAD - expert_total - 2), BF)
    packed = jnp.concatenate(
        [w_query, w_key, w_value, w_router, norm_attn[:, None], norm_moe[:, None], pad], axis=1
    )
    full = lax.all_gather(packed, "dp", axis=0, tiled=True)
    routes_low = jnp.concatenate(
        [routes.astype(BF), jnp.zeros((local_rows, PAD - TOP), BF)], axis=1
    )
    side_rows = jnp.concatenate([cotangent, routes_low], axis=1)
    sources = [lax.rem(me + count - s, count) for s in range(count)]
    key_pos = jnp.concatenate(
        [i * local_rows + jnp.arange(local_rows, dtype=jnp.int32) for i in sources]
    )
    cos, sin = rope_tables(key_pos)
    token_blocks, cot_down = [tokens], [side_rows]
    turned, weights = [], [w_gate, w_up, w_down]
    for step in range(1, count):
        up = upward(token_blocks[-1], "expert", count, 1, step - 1)
        down = downward(cot_down[-1], "expert", count, 1, step - 1)
        if weights:
            turned.append(jnp.transpose(weights.pop(0), (1, 0, 2)))
            up, down, turned, weights = lax.optimization_barrier((up, down, turned, weights))
        token_blocks.append(up)
        cot_down.append(down)
    wg, wu, wd = turned
    full, token_blocks, cot_down, w_out, cos, sin = lax.optimization_barrier(
        (full, token_blocks, cot_down, w_out, cos, sin)
    )
    out_full = lax.all_gather(w_out, "dp", axis=0, tiled=True)
    side_rows = cot_down[0]
    cot_up = [side_rows, upward(side_rows, "expert", count)]
    cot_up = cot_up + [upward(side_rows, "expert", count, s) for s in (2,) if count > 2]

    me_ref = jnp.stack([me, lax.axis_index("dp")]).astype(jnp.int32)
    normed_all, side, query, key, value, attended, lse = run_front(
        me_ref, token_blocks, full, cos, sin, query_width, key_width, expert_total
    )
    hidden = tokens.astype(F32)
    inverse_one = inverse_rms(hidden)
    gain_one = side[expert_total : expert_total + 1]
    gain_two = side[expert_total + 1 : expert_total + 2]
    router_full = full[:, qkv_width : qkv_width + expert_total]
    middle = hidden + RES_MULT * dot(attended, out_full)
    inverse_two = inverse_rms(middle)
    normed_two = (middle * inverse_two * gain_two).astype(BF)

    cot_up, cot_down, _ = lax.optimization_barrier((cot_up, cot_down, normed_two))
    while len(cot_up) < count:
        cot_up.append(upward(cot_up[-1], "expert", count, 1, len(cot_up) - 1))
    cot_blocks = [side_rows] + [cot_up[s] + cot_down[count - s] for s in range(1, count)]
    row = lax.broadcasted_iota(jnp.int32, (local_rows, local_rows), 0)
    col = lax.broadcasted_iota(jnp.int32, (local_rows, local_rows), 1)
    earlier = (row < col).astype(BF)
    all_ids = jnp.arange(expert_total, dtype=jnp.int32)
    own_ids = me * local_experts + jnp.arange(local_experts, dtype=jnp.int32)
    route_blocks, hots, hot_locals, places, cot_slots = [], [], [], [], []
    for s in range(count):
        named = cot_blocks[s][:, width : width + TOP].astype(F32).astype(jnp.int32)
        hot = jnp.any(named[:, :, None] == all_ids[None, None, :], axis=1)
        hot_local = jnp.any(
            named.T[None, :, :] == own_ids[:, None, None], axis=1
        )
        position = dot(hot_local.astype(BF), earlier).astype(jnp.int32)
        position = jnp.where(hot_local, position, -1)
        slots = jnp.arange(capacity, dtype=jnp.int32)
        place = (position[:, None, :] == slots[None, :, None]).astype(BF)
        place = place.reshape(local_experts * capacity, local_rows)
        hots.append(hot)
        hot_locals.append(hot_local)
        places.append(place)
        cot_slots.append(dot(place, cot_blocks[s][:, :width]).astype(BF))

    second_blocks = line_gather(normed_two, "expert", count)
    slot_rows, gates = [], []
    for s in range(count):
        logits = dot(second_blocks[s], router_full)
        masked = jnp.where(hots[s], logits, -1e30)
        exponent = jnp.where(
            hots[s], jnp.exp(masked - jnp.max(masked, axis=1, keepdims=True)), 0.0
        )
        gates.append(exponent / jnp.sum(exponent, axis=1, keepdims=True))
        slot_rows.append(dot(places[s], second_blocks[s]).astype(BF))
    gate_rows = jnp.stack(
        [lax.dynamic_slice_in_dim(g.T, me * local_experts, local_experts, 0) for g in gates],
        axis=1,
    )
    results, expert_sums = [], []
    for first, number in ((0, local_experts),):
        *results, grads = run_experts(
            me_ref,
            slot_rows,
            cot_slots,
            places,
            gate_rows,
            wg,
            wu,
            wd,
            slabs,
            expert_total,
            first,
            number,
            results,
        )
        expert_sums.append(lax.psum_scatter(grads, "dp", scatter_dimension=0, tiled=True))
    slot_outs, slot_backs = results[:count], results[count:]
    mix_parts = [dot(places[s], slot_outs[s], 0, 0).astype(BF) for s in range(count)]
    back_sum, (mix_parts, normed_t) = line_scatter(
        [dot(places[s], slot_backs[s], 0, 0).astype(BF) for s in range(count)],
        "expert",
        count,
        [mix_parts, normed_all.T],
    )

    gate_own = gates[0]
    weighted = (
        back_sum[:, width : width + expert_total]
        + back_sum[:, width + expert_total : width + 2 * expert_total]
    )
    grad_logits = (weighted - gate_own * jnp.sum(weighted, axis=1, keepdims=True)).astype(BF)
    grad_normed_two = back_sum[:, :width] + dot(grad_logits, router_full, 1, 1)
    grad_gain_two = jnp.sum(grad_normed_two * middle * inverse_two, axis=0, keepdims=True)
    grad_middle = cotangent.astype(F32) + norm_back(middle, inverse_two, gain_two, grad_normed_two)
    branch_back = (RES_MULT * grad_middle).astype(BF)
    logits_wide = jnp.pad(grad_logits, ((0, 0), (0, PAD - expert_total)))
    out_keep, out_send = run_out(
        me_ref, attended, branch_back, normed_two, logits_wide, grad_gain_two, slabs, expert_total
    )
    out_state = trade(out_keep, out_send, 0, slabs)
    mix_parts, out_state, branch_back = lax.optimization_barrier(
        (mix_parts, out_state, branch_back)
    )
    near = send_near(mix_parts, "expert", count)
    out_stages = slab_stages(out_state, slabs)
    out_halves = next(out_stages)
    query_pre, key_pre, value_pre, *qkv_grads = run_back(
        me_ref, branch_back, out_full, query, key, value, lse, cos, sin, normed_t, slabs
    )
    qkv_grads, key_pre, value_pre, near, out_halves = lax.optimization_barrier(
        (qkv_grads, key_pre, value_pre, near, out_halves)
    )
    key_value_parts = [
        jnp.concatenate(
            [x[s * local_rows : (s + 1) * local_rows] for x in (key_pre, value_pre)], axis=1
        )
        for s in range(count)
    ]
    key_value_came = [downward(key_value_parts[s], "expert", count, s) for s in range(1, count)]
    key_value_sum = [key_value_parts[0]]
    qkv_state = trade(*qkv_grads, 0, slabs)
    qkv_stages = slab_stages(qkv_state, slabs)
    qkv_halves = next(qkv_stages)
    for step in range(slabs.bit_length() - 3):
        out_halves = out_stages.send(out_halves)
        at = len(key_value_sum) - 1
        qkv_halves, out_halves, came = lax.optimization_barrier(
            (qkv_halves, out_halves, key_value_came[at : at + 2])
        )
        key_value_sum += came
        qkv_halves = qkv_stages.send(qkv_halves)
    left = key_value_came[len(key_value_sum) - 1 :]
    far, _ = lax.optimization_barrier((mix_parts[2:-1], key_value_sum[-1]))
    far = send_far(far, "expert", count)
    out_parts = own_parts(*out_halves, me, count)
    out_came = send_parts(out_parts, "expert", count)
    qkv_halves, left = lax.optimization_barrier((qkv_halves, left))
    key_value_sum = add_up(key_value_sum + left).astype(BF)
    out_sum = add_up(out_parts[:1] + out_came)
    qkv_parts = own_parts(*qkv_halves, me, count)
    qkv_sum = add_up(qkv_parts[:1] + send_parts(qkv_parts, "expert", count))
    output = (middle + add_up(mix_parts[:1] + near + far)).astype(BF)
    pairs = key_width // PAIR
    qkv_sum = qkv_sum.reshape(qkv_sum.shape[0], pairs, (GROUP + 2) * PAIR)
    wide = GROUP * PAIR
    qkv_sum = jnp.concatenate(
        [
            part.reshape(qkv_sum.shape[0], -1)
            for part in (
                qkv_sum[:, :, :wide],
                qkv_sum[:, :, wide : wide + PAIR],
                qkv_sum[:, :, wide + PAIR :],
            )
        ],
        axis=1,
    )
    grad_normed_one = dot(query_pre, full[:, :query_width], 1, 1) + dot(
        key_value_sum, full[:, query_width:qkv_width], 1, 1
    )
    grad_tokens = (grad_middle + norm_back(hidden, inverse_one, gain_one, grad_normed_one)).astype(
        BF
    )
    own = qkv_sum.shape[0]
    own_packed = lax.dynamic_slice_in_dim(packed, me * own, own, 0).astype(F32)
    gain_one_sum = (
        jnp.sum(own_packed[:, :qkv_width] * qkv_sum, axis=1)
        / own_packed[:, qkv_width + expert_total]
    )
    owned = [
        x.reshape(width // slabs, local_experts, x.shape[1]) for x in run_owned(expert_sums)
    ]
    return (
        output,
        grad_tokens,
        gain_one_sum,
        out_sum[:, width + expert_total],
        qkv_sum[:, :query_width],
        qkv_sum[:, query_width : query_width + key_width],
        qkv_sum[:, query_width + key_width :],
        out_sum[:, :width],
        out_sum[:, width : width + expert_total],
        *owned,
    )


def solution(mesh):
    rows = P(("dp", "expert"), None)
    in_specs = (
        [rows, rows, P("dp"), P("dp")]
        + [P("dp", None)] * 5
        + [P(None, "expert", None)] * 3
        + [rows]
    )
    out_specs = (
        [rows, rows, P(("dp", "expert")), P(("dp", "expert"))]
        + [rows] * 5
        + [P("dp", "expert", None)] * 3
    )
    return jax.shard_map(
        body, mesh=mesh, in_specs=tuple(in_specs), out_specs=tuple(out_specs), check_vma=False
    )
```

```python
import functools

import jax
import jax.numpy as jnp
from jax import lax
from jax.experimental import pallas as pl
from jax.experimental.pallas import tpu as pltpu
from jax.sharding import PartitionSpec as P

HEADS = 24
KV_HEADS = 8
HEAD_DIM = 64
TOP = 8
GROUP = HEADS // KV_HEADS
PAD = 128
PAIR = 2 * HEAD_DIM


RES_MULT = 0.22
ATT_MULT = 0.015625
NORM_EPS = 1e-06
ROPE_BASE = 10000.0
BF = jnp.bfloat16
F32 = jnp.float32


def dot(a, b, ca=1, cb=0):
    return lax.dot_general(a, b, (((ca,), (cb,)), ((), ())), preferred_element_type=F32)


def inverse_rms(hidden):
    return lax.rsqrt(jnp.mean(hidden * hidden, axis=-1, keepdims=True) + NORM_EPS)


def norm_back(hidden, inverse, gain_vector, grad_normed):
    weighted = grad_normed * gain_vector
    return inverse * weighted - hidden * inverse**3 * jnp.mean(
        weighted * hidden, axis=-1, keepdims=True
    )


def rope_tables(positions):
    half = HEAD_DIM // 2
    frequency = ROPE_BASE ** (-(jnp.arange(half, dtype=F32) * 2.0 / HEAD_DIM))
    angles = positions.astype(F32)[:, None] * frequency[None, :]
    cos, sin = jnp.cos(angles), jnp.sin(angles)
    return jnp.concatenate([cos] * 4, axis=1), jnp.concatenate([-sin, sin] * 2, axis=1)


def swap_halves(x):
    half = HEAD_DIM // 2
    lane = lax.broadcasted_iota(jnp.int32, x.shape, 1)
    return jnp.where(
        lane % HEAD_DIM < half, pltpu.roll(x, PAIR - half, 1), pltpu.roll(x, half, 1)
    )


def rope(x, cos, sin):
    return jnp.concatenate(
        [
            x[:, i : i + PAIR] * cos + swap_halves(x[:, i : i + PAIR]) * sin
            for i in range(0, x.shape[1], PAIR)
        ],
        axis=1,
    )


def causal_bias(me, count, rows):
    query = me * rows + lax.broadcasted_iota(jnp.int32, (rows, count * rows), 0)
    key = lax.broadcasted_iota(jnp.int32, (rows, count * rows), 1)
    source = me - key // rows
    source = jnp.where(source < 0, source + count, source)
    return jnp.where(source * rows + key % rows <= query, 0.0, -1e30)


def front_kernel(count, gain_at, me_ref, *refs):
    token_refs = refs[:count]
    wq_ref, wk_ref, wv_ref, side_ref, cos_ref, sin_ref = refs[count : count + 6]
    normed_ref, side_out, q_ref, k_ref, v_ref, att_ref, probs_ref, bias_ref = refs[count + 6 :]
    rows = token_refs[0].shape[0]

    @pl.when(pl.program_id(0) == 0)
    def _():
        side = side_ref[...].astype(F32).T
        side_out[...] = side
        for s in range(count):
            hidden = token_refs[s][...].astype(F32)
            normed = hidden * inverse_rms(hidden) * side[gain_at : gain_at + 1]
            normed_ref[s * rows : (s + 1) * rows] = normed.astype(BF)
        bias_ref[...] = causal_bias(me_ref[0], count, rows)

    cos, sin = cos_ref[...], sin_ref[...]
    query = rope(dot(normed_ref[:rows], wq_ref[...]), cos[:rows], sin[:rows]).astype(BF)
    query = query * ATT_MULT
    q_ref[...] = query
    both = dot(normed_ref[...], jnp.concatenate([wk_ref[...], wv_ref[...]], axis=1))
    key = rope(both[:, :PAIR], cos, sin).astype(BF)
    value = both[:, PAIR:].astype(BF)
    k_ref[...] = key
    v_ref[...] = value
    for head in range(2 * GROUP):
        at = slice(head * HEAD_DIM, (head + 1) * HEAD_DIM)
        kv_at = slice(head // GROUP * HEAD_DIM, (head // GROUP + 1) * HEAD_DIM)
        scores = dot(query[:, at], key[:, kv_at], 1, 1) + bias_ref[...]
        peak = jnp.max(scores, axis=1, keepdims=True)
        weight = jnp.exp(scores - peak)
        total = jnp.sum(weight, axis=1, keepdims=True)
        probs = (weight * (1.0 / total)).astype(BF)
        att_ref[:, at] = dot(probs, value[:, kv_at]).astype(BF)
        probs_ref[head * rows : (head + 1) * rows] = probs


def run_front(me, tokens, full, cos, sin, query_width, key_width, gain_at):
    count, (rows, width) = len(tokens), tokens[0].shape
    length, pairs, wide = count * rows, key_width // PAIR, GROUP * PAIR
    whole = lambda shape: pl.BlockSpec(shape, lambda p, i: (0, 0))
    column = lambda r, w, first: pl.BlockSpec((r, w), lambda p, i: (0, first + p))
    flops = 2 * width * (rows * query_width + 2 * length * key_width)
    flops += 4 * rows * length * query_width
    return pl.pallas_call(
        functools.partial(front_kernel, count, gain_at),
        grid_spec=pltpu.PrefetchScalarGridSpec(
            num_scalar_prefetch=1,
            grid=(pairs,),
            in_specs=[whole((rows, width))] * count
            + [
                column(width, wide, 0),
                column(width, PAIR, query_width // PAIR),
                column(width, PAIR, (query_width + key_width) // PAIR),
                pl.BlockSpec(
                    (width, PAIR), lambda p, i: (0, (query_width + 2 * key_width) // PAIR)
                ),
                whole((length, PAIR)),
                whole((length, PAIR)),
            ],
            out_specs=[
                whole((length, width)),
                whole((PAIR, width)),
                column(rows, wide, 0),
                column(length, PAIR, 0),
                column(length, PAIR, 0),
                column(rows, wide, 0),
                pl.BlockSpec((2 * GROUP * rows, length), lambda p, i: (p, 0)),
            ],
            scratch_shapes=[pltpu.VMEM((rows, length), F32)],
        ),
        out_shape=[
            jax.ShapeDtypeStruct((length, width), BF),
            jax.ShapeDtypeStruct((PAIR, width), F32),
            jax.ShapeDtypeStruct((rows, query_width), BF),
            jax.ShapeDtypeStruct((length, key_width), BF),
            jax.ShapeDtypeStruct((length, key_width), BF),
            jax.ShapeDtypeStruct((rows, query_width), BF),
            jax.ShapeDtypeStruct((pairs * 2 * GROUP * rows, length), BF),
        ],
        compiler_params=pltpu.CompilerParams(
            dimension_semantics=("arbitrary",), vmem_limit_bytes=56 * 2**20
        ),
        cost_estimate=pl.CostEstimate(
            flops=flops,
            bytes_accessed=4 * (length * width + full.size),
            transcendentals=rows * length * query_width // HEAD_DIM,
        ),
        name="front",
    )(me, *tokens, full, full, full, full, cos, sin)


def back_kernel(count, me_ref, *refs):
    branch_ref, wo_ref, q_ref, k_ref, v_ref, probs_ref, cos_ref, sin_ref, normed_ref = refs[:9]
    dq_ref, dk_ref, dv_ref, keep_ref, send_ref = refs[9:]
    rows = branch_ref.shape[0]
    grad = dot(branch_ref[...], wo_ref[...], 1, 1).astype(BF)
    query, key, value = q_ref[...], k_ref[...], v_ref[...]
    dqs, dks, dvs = [], [], []
    for head in range(2 * GROUP):
        at = slice(head * HEAD_DIM, (head + 1) * HEAD_DIM)
        kv_at = slice(head // GROUP * HEAD_DIM, (head // GROUP + 1) * HEAD_DIM)
        probs_low = probs_ref[head * rows : (head + 1) * rows]
        probs = probs_low.astype(F32)
        probs_back = dot(grad[:, at], value[:, kv_at], 1, 1)
        delta = jnp.sum(probs * probs_back, axis=1, keepdims=True)
        scores_back = (probs * (probs_back - delta)).astype(BF)
        dqs.append(dot(scores_back, key[:, kv_at]) * ATT_MULT)
        dk = dot(scores_back, query[:, at], 0, 0)
        dv = dot(probs_low, grad[:, at], 0, 0)
        if head % GROUP == 0:
            dks.append(dk)
            dvs.append(dv)
        else:
            dks[-1] = dks[-1] + dk
            dvs[-1] = dvs[-1] + dv
    cos, sin = cos_ref[...], sin_ref[...]
    dq = rope(jnp.concatenate(dqs, axis=1), cos[:rows], -sin[:rows]).astype(BF)
    dk = rope(jnp.concatenate(dks, axis=1), cos, -sin).astype(BF)
    dv = jnp.concatenate(dvs, axis=1).astype(BF)
    dq_ref[...] = dq
    dk_ref[...] = dk
    dv_ref[...] = dv
    wide = dq.shape[1]
    grad_q = dot(normed_ref[:, :rows], dq).astype(BF)
    grad_kv = dot(normed_ref[...], jnp.concatenate([dk, dv], axis=1)).astype(BF)
    store_slabs(keep_ref, send_ref, me_ref[1], slice(0, wide), grad_q)
    store_slabs(keep_ref, send_ref, me_ref[1], slice(wide, wide + 2 * PAIR), grad_kv)


def out_kernel(total, me_ref, att_ref, branch_ref, normed_ref, logit_ref, gain_ref, *grad_refs):
    width = branch_ref.shape[1]
    router = dot(normed_ref[...].T, logit_ref[...])
    gain = jnp.broadcast_to(gain_ref[0:1], (PAD, width)).T
    lane = lax.broadcasted_iota(jnp.int32, (width, PAD), 1)
    side = jnp.where(lane == total, gain, router).astype(BF)
    main = dot(att_ref[...].T, branch_ref[...]).astype(BF)
    store_slabs(*grad_refs, me_ref[1], slice(0, width), main)
    store_slabs(*grad_refs, me_ref[1], slice(width, width + PAD), side)


def run_out(me, attended, branch, normed, logits, gain, slabs, total):
    rows, width = branch.shape
    inner = attended.shape[1]
    spec = pl.BlockSpec(memory_space=pltpu.VMEM)
    return pl.pallas_call(
        functools.partial(out_kernel, total),
        in_specs=[pl.BlockSpec(memory_space=pltpu.SMEM)] + [spec] * 5,
        out_specs=[spec] * 2,
        out_shape=[jax.ShapeDtypeStruct((slabs // 2, inner // slabs, width + PAD), BF)] * 2,
        compiler_params=pltpu.CompilerParams(vmem_limit_bytes=48 * 2**20),
        cost_estimate=pl.CostEstimate(
            flops=2 * rows * inner * (width + PAD),
            bytes_accessed=2 * (3 * rows * width + inner * (width + PAD)),
            transcendentals=0,
        ),
        name="out_grad",
    )(me, attended, branch, normed, logits, gain)


def run_back(me, branch, out_full, query, key, value, probs, cos, sin, normed_t, slabs):
    (rows, width), (length, key_width) = branch.shape, key.shape
    count, pairs, wide = length // rows, key_width // PAIR, GROUP * PAIR
    whole = lambda shape: pl.BlockSpec(shape, lambda p, i: (0, 0))
    column = lambda r, w: pl.BlockSpec((r, w), lambda p, i: (0, p))
    flops = 2 * width * (2 * rows * query.shape[1] + 2 * length * key_width)
    flops += 8 * rows * length * query.shape[1]
    return pl.pallas_call(
        functools.partial(back_kernel, count),
        grid_spec=pltpu.PrefetchScalarGridSpec(
            num_scalar_prefetch=1,
            grid=(pairs,),
            in_specs=[
                whole((rows, width)),
                pl.BlockSpec((wide, width), lambda p, i: (p, 0)),
                column(rows, wide),
                column(length, PAIR),
                column(length, PAIR),
                pl.BlockSpec((2 * GROUP * rows, length), lambda p, i: (p, 0)),
                whole((length, PAIR)),
                whole((length, PAIR)),
                whole((width, length)),
            ],
            out_specs=[
                column(rows, wide),
                column(length, PAIR),
                column(length, PAIR),
            ]
            + [pl.BlockSpec((slabs // 2, width // slabs, wide + 2 * PAIR), lambda p, i: (0, 0, p))]
            * 2,
        ),
        out_shape=[
            jax.ShapeDtypeStruct(query.shape, BF),
            jax.ShapeDtypeStruct(key.shape, BF),
            jax.ShapeDtypeStruct(key.shape, BF),
        ]
        + [jax.ShapeDtypeStruct((slabs // 2, width // slabs, pairs * (wide + 2 * PAIR)), BF)] * 2,
        compiler_params=pltpu.CompilerParams(
            dimension_semantics=("arbitrary",), vmem_limit_bytes=56 * 2**20
        ),
        cost_estimate=pl.CostEstimate(
            flops=flops,
            bytes_accessed=2 * (length * width + 2 * width * query.shape[1] + probs.size),
            transcendentals=0,
        ),
        name="back",
    )(me, branch, out_full, query, key, value, probs, cos, sin, normed_t)


def line_gather(block, axis, count):
    right, left = [block], [block]
    for step in range(1, count):
        right.append(
            lax.ppermute(right[-1], axis, [(i, i + 1) for i in range(step - 1, count - 1)])
        )
        left.append(lax.ppermute(left[-1], axis, [(i, i - 1) for i in range(1, count - step + 1)]))
    return [block] + [right[s] + left[count - s] for s in range(1, count)]


def line_scatter(parts, axis, count, beside):
    if count == 1:
        return parts[0].astype(F32), beside
    right, left, ready = parts[1], parts[count - 1], []
    for step in range(1, count):
        right = lax.ppermute(right, axis, [(i, i + 1) for i in range(step)])
        left = lax.ppermute(left, axis, [(i, i - 1) for i in range(count - step, count)])
        if beside:
            right, left, now = lax.optimization_barrier((right, left, beside.pop(0)))
            ready.append(now)
        if step < count - 1:
            right = parts[step + 1] + right
            left = parts[count - 1 - step] + left
    return parts[0].astype(F32) + right.astype(F32) + left.astype(F32), ready + beside


def upward(block, axis, count, distance=1, first=0):
    pairs = [(i, i + distance) for i in range(first, count - distance)]
    return lax.ppermute(block, axis, pairs)


def downward(block, axis, count, distance=1, last=0):
    pairs = [(i, i - distance) for i in range(distance, count - last)]
    return lax.ppermute(block, axis, pairs)


def send_parts(parts, axis, count):
    return [
        lax.ppermute(parts[s], axis, [(i, (i + count - s) % count) for i in range(count)])
        for s in range(1, count)
    ]


def send_near(parts, axis, count):
    shifts = [s for s in {1: 1, count - 1: 1} if 0 < s < count]
    return [
        lax.ppermute(parts[s], axis, [(i, (i + count - s) % count) for i in range(count)])
        for s in shifts
    ]


def send_far(parts, axis, count):
    return [
        lax.ppermute(part, axis, [(i, (i + count - s) % count) for i in range(count)])
        for s, part in enumerate(parts, 2)
    ]


def add_up(parts):
    total = parts[0].astype(F32)
    for part in parts[1:]:
        total = total + part.astype(F32)
    return total


def trade(keep, send, bit, slabs):
    return keep + lax.ppermute(send, "dp", [(i, i ^ (1 << bit)) for i in range(slabs)])


def halve(x, bits, bit, slabs):
    at = bits.index(bit)
    keep, send = (lax.index_in_dim(x, i, at, False) for i in (0, 1))
    return trade(keep, send, bit, slabs), [b for b in bits if b != bit]


def slab_stages(x, slabs):
    top = slabs.bit_length() - 1
    bits = list(range(top - 1, 0, -1))
    x = x.reshape((2,) * (top - 1) + x.shape[1:])
    one, two = jnp.split(x, 2, axis=len(bits))
    bits_one, bits_two = bits, bits
    for k in range(len(bits)):
        one, bits_one = halve(one, bits_one, k + 1, slabs)
        two, bits_two = halve(two, bits_two, len(bits) - k, slabs)
        one, two = yield one, two


def own_parts(one, two, me, count):
    x = jnp.concatenate([one, two], axis=0)
    own = x.shape[0] // count
    return [
        lax.dynamic_slice_in_dim(x, lax.rem(me + count - s, count) * own, own, 0)
        for s in range(count)
    ]


def store_slabs(keep_ref, send_ref, own, at, value):
    half, slab, _ = keep_ref.shape
    for odd in (0, 1):

        @pl.when(lax.rem(own, 2) == odd)
        def _():
            for d in range(2 * half):
                ref = keep_ref if d % 2 == odd else send_ref
                place = lax.bitwise_xor(jnp.int32(d), own) // 2
                ref[place, :, at] = value[d * slab : (d + 1) * slab]


def expert_kernel(count, total, experts, first, me_ref, *refs):
    x_refs, g_refs, p_refs = refs[:count], refs[count : 2 * count], refs[2 * count : 3 * count]
    gate_refs, (wg_ref, wu_ref, wd_ref) = refs[3 * count : 4 * count], refs[4 * count : 4 * count + 3]
    outs = refs[-2 * count - 1 :]
    out_refs, back_refs, grads_ref = outs[:count], outs[count : 2 * count], outs[2 * count]
    capacity, width = x_refs[0].shape
    local = first + pl.program_id(0)
    expert = me_ref[0] * experts + local
    x = jnp.concatenate([r[...] for r in x_refs], axis=0)
    g = jnp.concatenate([r[...] for r in g_refs], axis=0)
    gate = jnp.concatenate(
        [
            jnp.sum(p_ref[...].astype(F32) * gate_ref[pl.ds(local, 1), :], axis=1, keepdims=True)
            for p_ref, gate_ref in zip(p_refs, gate_refs)
        ],
        axis=0,
    )
    wg, wu, wd = wg_ref[0], wu_ref[0], wd_ref[0]
    gate_pre = dot(x, wg)
    up_pre = dot(x, wu)
    back_active = dot(g, wd)
    sig = 1.0 / (1.0 + jnp.exp(-gate_pre))
    silu = gate_pre * sig
    active = silu * up_pre
    slot_gate = RES_MULT * gate
    gate_grad = slot_gate * jnp.sum(active * back_active, axis=1, keepdims=True)
    active_low = (active * slot_gate).astype(BF)
    back_active = back_active * slot_gate
    gate_back = (back_active * up_pre * sig * (1.0 + gate_pre * (1.0 - sig))).astype(BF)
    up_back = (back_active * silu).astype(BF)
    out = dot(active_low, wd, 1, 1).astype(BF)
    back = (dot(gate_back, wg, 1, 1) + dot(up_back, wu, 1, 1)).astype(BF)
    lane = lax.broadcasted_iota(jnp.int32, (gate_grad.shape[0], PAD), 1)
    high = gate_grad.astype(BF).astype(F32)
    extra = jnp.where(
        lane == expert, high, jnp.where(lane == total + expert, gate_grad - high, 0.0)
    ).astype(BF)
    for s in range(count):
        rows = slice(s * capacity, (s + 1) * capacity)
        out_refs[s][...] = out[rows]
        back_refs[s][:, :width] = back[rows]
        back_refs[s][:, width:] = extra[rows]
    slabs, rows = grads_ref.shape[0], grads_ref.shape[3]
    for k, (a, b) in enumerate(((x, gate_back), (x, up_back), (g, active_low))):
        grads_ref[:, k, 0] = dot(a, b, 0, 0).astype(BF).reshape(slabs, rows, b.shape[1])


def run_experts(index, xs, gs, places, gates, wg, wu, wd, slabs, total, first, number, earlier):
    count = len(xs)
    experts, width, hidden = wg.shape
    capacity = xs[0].shape[0] // experts
    block = lambda w: pl.BlockSpec((capacity, w), lambda e, i: (first + e, 0))
    weight = pl.BlockSpec((1, width, hidden), lambda e, i: (first + e, 0, 0))
    rows = width // slabs
    slots = count * number * capacity
    inputs = [*xs, *gs, *places, *gates, wg, wu, wd, *earlier]
    return pl.pallas_call(
        functools.partial(expert_kernel, count, total, experts, first),
        grid_spec=pltpu.PrefetchScalarGridSpec(
            num_scalar_prefetch=1,
            grid=(number,),
            in_specs=[block(width)] * (2 * count)
            + [block(places[0].shape[1])] * count
            + [pl.BlockSpec(gates[0].shape, lambda e, i: (0, 0))] * count
            + [weight] * 3
            + [pl.BlockSpec(memory_space=pl.ANY)] * len(earlier),
            out_specs=[block(width)] * count
            + [block(width + PAD)] * count
            + [pl.BlockSpec((slabs, 3, 1, rows, hidden), lambda e, i: (0, 0, e, 0, 0))],
        ),
        out_shape=[jax.ShapeDtypeStruct((experts * capacity, width), BF)] * count
        + [jax.ShapeDtypeStruct((experts * capacity, width + PAD), BF)] * count
        + [jax.ShapeDtypeStruct((slabs, 3, number, rows, hidden), BF)],
        input_output_aliases={1 + len(inputs) - len(earlier) + i: i for i in range(len(earlier))},
        compiler_params=pltpu.CompilerParams(
            dimension_semantics=("arbitrary",), vmem_limit_bytes=60 * 2**20
        ),
        cost_estimate=pl.CostEstimate(
            flops=18 * slots * width * hidden,
            bytes_accessed=2 * (4 * slots * width + 6 * number * width * hidden),
            transcendentals=slots * hidden,
        ),
        name="experts",
    )(index, *inputs)


def owned_kernel(*refs):
    owned, sums = refs[-3:], refs[:-3]
    experts = sum(ref.shape[2] for ref in sums)
    at = 0
    for ref in sums:
        for e in range(ref.shape[2]):
            for k, out in enumerate(owned):
                out[pl.ds(at, ref.shape[3], stride=experts), :] = ref[0, k, e].astype(F32)
            at += 1


def run_owned(sums):
    rows, hidden = sums[0].shape[3:]
    experts = sum(x.shape[2] for x in sums)
    lanes = 128
    return pl.pallas_call(
        owned_kernel,
        grid=(hidden // lanes,),
        in_specs=[
            pl.BlockSpec((1, 3, x.shape[2], rows, lanes), lambda i: (0, 0, 0, 0, i)) for x in sums
        ],
        out_specs=[pl.BlockSpec((rows * experts, lanes), lambda i: (0, i))] * 3,
        out_shape=[jax.ShapeDtypeStruct((rows * experts, hidden), F32)] * 3,
        compiler_params=pltpu.CompilerParams(
            dimension_semantics=("arbitrary",), vmem_limit_bytes=32 * 2**20
        ),
        cost_estimate=pl.CostEstimate(
            flops=0, bytes_accessed=18 * rows * experts * hidden, transcendentals=0
        ),
        name="owned",
    )(*sums)


def body(
    tokens,
    cotangent,
    norm_attn,
    norm_moe,
    w_query,
    w_key,
    w_value,
    w_out,
    w_router,
    w_gate,
    w_up,
    w_down,
    routes,
):
    local_rows, width = tokens.shape
    count = lax.axis_size("expert")
    slabs = lax.axis_size("dp")
    local_experts = w_gate.shape[1]
    expert_total = local_experts * count
    capacity = min(local_rows, max(2, local_rows * TOP * 7 // (4 * expert_total)))
    capacity = -(-capacity // 16) * 16
    query_width = w_query.shape[1]
    key_width = w_key.shape[1]
    qkv_width = query_width + 2 * key_width
    me = lax.axis_index("expert")

    pad = jnp.zeros((width // slabs, PAD - expert_total - 2), BF)
    packed = jnp.concatenate(
        [w_query, w_key, w_value, w_router, norm_attn[:, None], norm_moe[:, None], pad], axis=1
    )
    full = lax.all_gather(packed, "dp", axis=0, tiled=True)
    routes_low = jnp.concatenate(
        [routes.astype(BF), jnp.zeros((local_rows, PAD - TOP), BF)], axis=1
    )
    side_rows = jnp.concatenate([cotangent, routes_low], axis=1)
    sources = [lax.rem(me + count - s, count) for s in range(count)]
    key_pos = jnp.concatenate(
        [i * local_rows + jnp.arange(local_rows, dtype=jnp.int32) for i in sources]
    )
    cos, sin = rope_tables(key_pos)
    token_blocks, cot_down = [tokens], [side_rows]
    turned, weights = [], [w_gate, w_up, w_down]
    for step in range(1, count):
        up = upward(token_blocks[-1], "expert", count, 1, step - 1)
        down = downward(cot_down[-1], "expert", count, 1, step - 1)
        if weights:
            turned.append(jnp.transpose(weights.pop(0), (1, 0, 2)))
            up, down, turned, weights = lax.optimization_barrier((up, down, turned, weights))
        token_blocks.append(up)
        cot_down.append(down)
    wg, wu, wd = turned
    full, token_blocks, cot_down, w_out, cos, sin = lax.optimization_barrier(
        (full, token_blocks, cot_down, w_out, cos, sin)
    )
    out_full = lax.all_gather(w_out, "dp", axis=0, tiled=True)
    side_rows = cot_down[0]
    cot_up = [side_rows, upward(side_rows, "expert", count)]
    cot_up = cot_up + [upward(side_rows, "expert", count, s) for s in (2,) if count > 2]

    me_ref = jnp.stack([me, lax.axis_index("dp")]).astype(jnp.int32)
    normed_all, side, query, key, value, attended, probs = run_front(
        me_ref, token_blocks, full, cos, sin, query_width, key_width, expert_total
    )
    hidden = tokens.astype(F32)
    inverse_one = inverse_rms(hidden)
    gain_one = side[expert_total : expert_total + 1]
    gain_two = side[expert_total + 1 : expert_total + 2]
    router_full = full[:, qkv_width : qkv_width + expert_total]
    middle = hidden + RES_MULT * dot(attended, out_full)
    inverse_two = inverse_rms(middle)
    normed_two = (middle * inverse_two * gain_two).astype(BF)

    cot_up, cot_down, _ = lax.optimization_barrier((cot_up, cot_down, normed_two))
    while len(cot_up) < count:
        cot_up.append(upward(cot_up[-1], "expert", count, 1, len(cot_up) - 1))
    cot_blocks = [side_rows] + [cot_up[s] + cot_down[count - s] for s in range(1, count)]
    row = lax.broadcasted_iota(jnp.int32, (local_rows, local_rows), 0)
    col = lax.broadcasted_iota(jnp.int32, (local_rows, local_rows), 1)
    earlier = (row < col).astype(BF)
    all_ids = jnp.arange(expert_total, dtype=jnp.int32)
    own_ids = me * local_experts + jnp.arange(local_experts, dtype=jnp.int32)
    route_blocks, hots, hot_locals, places, cot_slots = [], [], [], [], []
    for s in range(count):
        named = cot_blocks[s][:, width : width + TOP].astype(F32).astype(jnp.int32)
        hot = jnp.any(named[:, :, None] == all_ids[None, None, :], axis=1)
        hot_local = jnp.any(
            named.T[None, :, :] == own_ids[:, None, None], axis=1
        )
        position = dot(hot_local.astype(BF), earlier).astype(jnp.int32)
        position = jnp.where(hot_local, position, -1)
        slots = jnp.arange(capacity, dtype=jnp.int32)
        place = (position[:, None, :] == slots[None, :, None]).astype(BF)
        place = place.reshape(local_experts * capacity, local_rows)
        hots.append(hot)
        hot_locals.append(hot_local)
        places.append(place)
        cot_slots.append(dot(place, cot_blocks[s][:, :width]).astype(BF))

    second_blocks = line_gather(normed_two, "expert", count)
    slot_rows, gates = [], []
    for s in range(count):
        logits = dot(second_blocks[s], router_full)
        masked = jnp.where(hots[s], logits, -1e30)
        exponent = jnp.where(
            hots[s], jnp.exp(masked - jnp.max(masked, axis=1, keepdims=True)), 0.0
        )
        gates.append(exponent / jnp.sum(exponent, axis=1, keepdims=True))
        slot_rows.append(dot(places[s], second_blocks[s]).astype(BF))
    gate_rows = [
        lax.dynamic_slice_in_dim(g.T, me * local_experts, local_experts, 0) for g in gates
    ]
    results, expert_sums = [], []
    early = max(1, local_experts // 4)
    for first, number in ((0, early), (early, local_experts - early)):
        *results, grads = run_experts(
            me_ref,
            slot_rows,
            cot_slots,
            places,
            gate_rows,
            wg,
            wu,
            wd,
            slabs,
            expert_total,
            first,
            number,
            results,
        )
        expert_sums.append(lax.psum_scatter(grads, "dp", scatter_dimension=0, tiled=True))
    slot_outs, slot_backs = results[:count], results[count:]
    mix_parts = [dot(places[s], slot_outs[s], 0, 0).astype(BF) for s in range(count)]
    back_sum, (mix_parts, normed_t) = line_scatter(
        [dot(places[s], slot_backs[s], 0, 0).astype(BF) for s in range(count)],
        "expert",
        count,
        [mix_parts, normed_all.T],
    )

    gate_own = gates[0]
    weighted = (
        back_sum[:, width : width + expert_total]
        + back_sum[:, width + expert_total : width + 2 * expert_total]
    )
    grad_logits = (weighted - gate_own * jnp.sum(weighted, axis=1, keepdims=True)).astype(BF)
    grad_normed_two = back_sum[:, :width] + dot(grad_logits, router_full, 1, 1)
    grad_gain_two = jnp.sum(grad_normed_two * middle * inverse_two, axis=0, keepdims=True)
    grad_middle = cotangent.astype(F32) + norm_back(middle, inverse_two, gain_two, grad_normed_two)
    branch_back = (RES_MULT * grad_middle).astype(BF)
    logits_wide = jnp.pad(grad_logits, ((0, 0), (0, PAD - expert_total)))
    out_keep, out_send = run_out(
        me_ref, attended, branch_back, normed_two, logits_wide, grad_gain_two, slabs, expert_total
    )
    out_state = trade(out_keep, out_send, 0, slabs)
    mix_parts, out_state, branch_back = lax.optimization_barrier(
        (mix_parts, out_state, branch_back)
    )
    near = send_near(mix_parts, "expert", count)
    out_stages = slab_stages(out_state, slabs)
    out_halves = next(out_stages)
    query_pre, key_pre, value_pre, *qkv_grads = run_back(
        me_ref, branch_back, out_full, query, key, value, probs, cos, sin, normed_t, slabs
    )
    qkv_grads, key_pre, value_pre, near, out_halves = lax.optimization_barrier(
        (qkv_grads, key_pre, value_pre, near, out_halves)
    )
    key_value_parts = [
        jnp.concatenate(
            [x[s * local_rows : (s + 1) * local_rows] for x in (key_pre, value_pre)], axis=1
        )
        for s in range(count)
    ]
    key_value_came = [downward(key_value_parts[s], "expert", count, s) for s in range(1, count)]
    key_value_sum = [key_value_parts[0]]
    qkv_state = trade(*qkv_grads, 0, slabs)
    qkv_stages = slab_stages(qkv_state, slabs)
    qkv_halves = next(qkv_stages)
    for step in range(slabs.bit_length() - 3):
        out_halves = out_stages.send(out_halves)
        at = len(key_value_sum) - 1
        qkv_halves, out_halves, came = lax.optimization_barrier(
            (qkv_halves, out_halves, key_value_came[at : at + 2])
        )
        key_value_sum += came
        qkv_halves = qkv_stages.send(qkv_halves)
    left = key_value_came[len(key_value_sum) - 1 :]
    far, _ = lax.optimization_barrier((mix_parts[2:-1], key_value_sum[-1]))
    far = send_far(far, "expert", count)
    out_parts = own_parts(*out_halves, me, count)
    out_came = send_parts(out_parts, "expert", count)
    qkv_halves, left = lax.optimization_barrier((qkv_halves, left))
    key_value_sum = add_up(key_value_sum + left).astype(BF)
    out_sum = add_up(out_parts[:1] + out_came)
    qkv_parts = own_parts(*qkv_halves, me, count)
    qkv_sum = add_up(qkv_parts[:1] + send_parts(qkv_parts, "expert", count))
    output = (middle + add_up(mix_parts[:1] + near + far)).astype(BF)
    pairs = key_width // PAIR
    qkv_sum = qkv_sum.reshape(qkv_sum.shape[0], pairs, (GROUP + 2) * PAIR)
    wide = GROUP * PAIR
    qkv_sum = jnp.concatenate(
        [
            part.reshape(qkv_sum.shape[0], -1)
            for part in (
                qkv_sum[:, :, :wide],
                qkv_sum[:, :, wide : wide + PAIR],
                qkv_sum[:, :, wide + PAIR :],
            )
        ],
        axis=1,
    )
    grad_normed_one = dot(query_pre, full[:, :query_width], 1, 1) + dot(
        key_value_sum, full[:, query_width:qkv_width], 1, 1
    )
    grad_tokens = (grad_middle + norm_back(hidden, inverse_one, gain_one, grad_normed_one)).astype(
        BF
    )
    own = qkv_sum.shape[0]
    own_packed = lax.dynamic_slice_in_dim(packed, me * own, own, 0).astype(F32)
    gain_one_sum = (
        jnp.sum(own_packed[:, :qkv_width] * qkv_sum, axis=1)
        / own_packed[:, qkv_width + expert_total]
    )
    owned = [
        x.reshape(width // slabs, local_experts, x.shape[1]) for x in run_owned(expert_sums)
    ]
    return (
        output,
        grad_tokens,
        gain_one_sum,
        out_sum[:, width + expert_total],
        qkv_sum[:, :query_width],
        qkv_sum[:, query_width : query_width + key_width],
        qkv_sum[:, query_width + key_width :],
        out_sum[:, :width],
        out_sum[:, width : width + expert_total],
        *owned,
    )


def solution(mesh):
    rows = P(("dp", "expert"), None)
    in_specs = (
        [rows, rows, P("dp"), P("dp")]
        + [P("dp", None)] * 5
        + [P(None, "expert", None)] * 3
        + [rows]
    )
    out_specs = (
        [rows, rows, P(("dp", "expert")), P(("dp", "expert"))]
        + [rows] * 5
        + [P("dp", "expert", None)] * 3
    )
    return jax.shard_map(
        body, mesh=mesh, in_specs=tuple(in_specs), out_specs=tuple(out_specs), check_vma=False
    )
```
